512 devices in a mesh: dp: 16 (over z, core), expert: 32 (over y, x).
Axes of the slice: x: 4, y: 8, z: 8, core: 2. Of those that a mesh axis runs over, the one named last changes fastest.
Arguments:
- tokens: bfloat16 [16384, 4096], P('expert', 'dp'), may hold values from -6 to 6
- cotangent: bfloat16 [16384, 4096], P('expert', 'dp'), may hold values from -6 to 6
- route: int32 [16384, 8], P('expert'), may hold values from 0 to 255, all different within a row
- prob: float32 [16384, 8], P('expert'), may hold values from 0.05 to 0.5
- quota: int32 [32], replicated, may hold values from 8 to 24, as said below
- w_gate: bfloat16 [32, 4096, 1024], P('expert', 'dp'), may hold values from -0.09375 to 0.09375
- w_up: bfloat16 [32, 4096, 1024], P('expert', 'dp'), may hold values from -0.09375 to 0.09375
- w_down: bfloat16 [32, 1024, 4096], P('expert', None, 'dp'), may hold values from -0.1875 to 0.1875
Outputs:
- mixed: bfloat16 [16384, 4096], P('expert', 'dp')
- grad_tokens: bfloat16 [16384, 4096], P('expert', 'dp')
- grad_gate: bfloat16 [32, 4096, 1024], P('expert', 'dp')
- grad_up: bfloat16 [32, 4096, 1024], P('expert', 'dp')
- grad_down: bfloat16 [32, 1024, 4096], P('expert', None, 'dp')
The draws below stay inside these ranges and needn't reach their ends.
Inputs may be any that keep to these rules, and one draw needn't show every extreme that they name: `route`: each row names 8 different experts. quota[e] + quota[e + 16] = 32 for every e below 16.
All inputs are finite; a program needn't handle non-finite values.
Results may differ from the reference program's by a relative error of at most 0.035.
Values may be sent and summed in bfloat16 or wider, within the bound.
A program may use at most 64 MiB of HBM per device.

```python
import math
import jax
import jax.numpy as jnp
from jax import lax

D = 4096
H = 1024
EXPERTS = 256
TOPK = 8
TOKJ = 512
WIN = 32
TOKENS = 16384
BASE = 16
SPREAD = 8
QHI = 24
N_DP = 16


def draw_quota(key, part):
    key = jax.random.fold_in(key, 7)
    first_key, second_key = jax.random.split(key)
    half_count = WIN // 2
    shifts = jax.random.randint(first_key, (half_count,), -SPREAD, SPREAD + 1)
    picked = jax.random.randint(second_key, (), 0, half_count)
    pair_ids = jnp.arange(half_count, dtype=jnp.int32)
    shifts = jnp.where(pair_ids == picked, SPREAD, shifts)
    return jnp.concatenate([BASE + shifts, BASE - shifts]).astype(jnp.int32)


def block_scale(own_key, shape, shards, low, high):
    loudness = 1.0
    for dim, shards_of in shards:
        heights = jax.random.uniform(jax.random.fold_in(jax.random.fold_in(own_key, 6), dim), (shards_of,), jnp.float32, low / len(shards), high / len(shards))
        loudness = loudness * jnp.repeat(jnp.exp(heights), shape[dim] // shards_of).reshape((-1,) + (1,) * (len(shape) - 1 - dim))
    return loudness


def picks_of(stream_key, rows, amount, top, lift):
    ranking = jax.random.permutation(jax.random.fold_in(stream_key, 1), amount)
    pull = ranking
    for power in range(3):
        pull = pull * pull // amount
    pull = pull * lift // amount
    lots = jax.random.randint(jax.random.fold_in(stream_key, 2), (rows, amount), 0, 4096) + pull
    holders = jax.random.permutation(jax.random.fold_in(stream_key, 3), rows)[jnp.arange(amount) % rows]
    lots = jnp.where(jnp.arange(rows)[:, None] == holders[None, :], 1 << 14, lots)
    priority = lots * amount + jnp.arange(amount)
    return lax.top_k(priority.astype(jnp.int32), top)[1].astype(jnp.int32)


def gaussian(key, extent, scale, limit, cuts=(), held_as=jnp.bfloat16):
    drawn = jax.random.normal(key, extent, jnp.float32) * scale
    if len(cuts) > 0:
        drawn = block_scale(key, extent, cuts, -0.22, 0.18) * drawn
    return jnp.clip(drawn, min=-limit, max=limit).astype(held_as)


def setup_inputs(seed: int = 0) -> dict:
    key_of = jax.random.split(jax.random.key(seed), 9)
    return {
        "tokens": gaussian(key_of[0], (TOKENS, D), 1.0, 6.0, ((0, 32), (1, 16))),
        "cotangent": gaussian(key_of[1], (TOKENS, D), 1.0, 6.0, ((0, 32), (1, 16))),
        "route": picks_of(key_of[2], TOKENS, EXPERTS, TOPK, 512),
        "prob": jnp.clip(jnp.exp(math.log(0.5) - 2.3025851 * jax.random.uniform(key_of[3], (TOKENS, TOPK), jnp.float32) ** block_scale(key_of[3], (TOKENS, TOPK), ((0, 32),), -0.2, 0.2)), 0.05, 0.5),
        "quota": draw_quota(jax.random.fold_in(key_of[8], 71), 0),
        "w_gate": gaussian(key_of[5], (WIN, D, H), D ** -0.5, 0.09375, ((0, 32), (1, 16))),
        "w_up": gaussian(key_of[6], (WIN, D, H), D ** -0.5, 0.09375, ((0, 32), (1, 16))),
        "w_down": gaussian(key_of[7], (WIN, H, D), H ** -0.5, 0.1875, ((0, 32), (2, 16))),
    }


def block_sum(left_side, right_blocks, pattern, row_total):
    blocks = left_side.reshape(row_total, N_DP, -1).astype(jnp.float32)
    block_parts = jnp.einsum(pattern, blocks, right_blocks.astype(jnp.float32))
    block_parts = lax.optimization_barrier(block_parts.astype(jnp.bfloat16)).astype(jnp.float32)
    return jnp.sum(block_parts, axis=0)


def reference(tokens, cotangent, route, prob, quota, w_gate, w_up, w_down):
    model_width = tokens.shape[1]
    block_width = model_width // N_DP
    hidden_width = w_gate.shape[2]
    row_total = WIN * QHI
    columns = route.reshape(WIN, TOKJ, TOPK)
    expert_ids = jnp.arange(WIN, dtype=jnp.int32)
    matches = (columns[..., None] == expert_ids).astype(jnp.int32)
    per_token = jnp.sum(matches, axis=2)
    before = jnp.cumsum(per_token, axis=1) - per_token
    position = jnp.sum(matches * before[:, :, None, :], axis=3)
    in_window = columns < WIN
    safe_route = jnp.where(in_window, columns, 0)
    served = in_window & (position < quota[safe_route])
    column_ids = jnp.arange(WIN, dtype=jnp.int32)[:, None, None]
    token_ids = column_ids * TOKJ + jnp.arange(TOKJ, dtype=jnp.int32)[None, :, None]
    flat_served = served.reshape(-1)
    flat_route = columns.reshape(-1)
    flat_row = (column_ids * QHI + position).reshape(-1).astype(jnp.int32)
    flat_token = jnp.broadcast_to(token_ids, columns.shape).reshape(-1).astype(jnp.int32)
    flat_prob = prob.reshape(-1)
    token_pad = jnp.concatenate([tokens, jnp.zeros((1, model_width), tokens.dtype)], axis=0)
    grad_pad = jnp.concatenate([cotangent.astype(jnp.float32), jnp.zeros((1, model_width), jnp.float32)], axis=0)
    contract_rows = (((0,), (0,)), ((), ()))
    contract_cols = (((1,), (1,)), ((), ()))

    def one_expert(totals, expert):
        mixed_acc, back_acc = totals
        chosen = flat_served & (flat_route == expert)
        target = jnp.where(chosen, flat_row, row_total).astype(jnp.int32)
        slot_token = jnp.full((row_total,), TOKENS, jnp.int32).at[target].set(flat_token, mode="drop")
        slot_prob = jnp.zeros((row_total,), jnp.float32).at[target].set(flat_prob, mode="drop")
        slot_rows = token_pad[slot_token]
        slot_grads = (slot_prob[:, None] * grad_pad[slot_token]).astype(jnp.bfloat16)
        gate_matrix = w_gate[expert]
        up_matrix = w_up[expert]
        down_matrix = w_down[expert]
        gate_pre = block_sum(slot_rows, gate_matrix.reshape(N_DP, block_width, hidden_width), "rbd,bdh->brh", row_total)
        up_pre = block_sum(slot_rows, up_matrix.reshape(N_DP, block_width, hidden_width), "rbd,bdh->brh", row_total)
        back_hidden = block_sum(slot_grads, down_matrix.reshape(hidden_width, N_DP, block_width), "rbd,hbd->brh", row_total)
        sigmoid_g = jax.nn.sigmoid(gate_pre)
        active = gate_pre * sigmoid_g
        hidden = (active * up_pre).astype(jnp.bfloat16)
        grad_pre = (back_hidden * up_pre * sigmoid_g * (1.0 + gate_pre * (1.0 - sigmoid_g))).astype(jnp.bfloat16)
        grad_up_pre = (back_hidden * active).astype(jnp.bfloat16)
        expert_out = jnp.dot(hidden, down_matrix, preferred_element_type=jnp.float32).astype(jnp.bfloat16)
        back_rows = lax.dot_general(grad_pre, gate_matrix, contract_cols, preferred_element_type=jnp.float32)
        back_rows = back_rows + lax.dot_general(grad_up_pre, up_matrix, contract_cols, preferred_element_type=jnp.float32)
        back_rows = back_rows.astype(jnp.bfloat16)
        grad_gate = lax.dot_general(slot_rows, grad_pre, contract_rows, preferred_element_type=jnp.float32).astype(jnp.bfloat16)
        grad_up = lax.dot_general(slot_rows, grad_up_pre, contract_rows, preferred_element_type=jnp.float32).astype(jnp.bfloat16)
        grad_down = lax.dot_general(hidden, slot_grads, contract_rows, preferred_element_type=jnp.float32).astype(jnp.bfloat16)
        mixed_acc = mixed_acc.at[slot_token].add(slot_prob[:, None] * expert_out.astype(jnp.float32), mode="drop")
        back_acc = back_acc.at[slot_token].add(back_rows.astype(jnp.float32), mode="drop")
        return (mixed_acc, back_acc), (grad_gate, grad_up, grad_down)

    start_sums = (jnp.zeros((TOKENS, model_width), jnp.float32), jnp.zeros((TOKENS, model_width), jnp.float32))
    (mixed_acc, back_acc), (grad_gate, grad_up, grad_down) = lax.scan(one_expert, start_sums, jnp.arange(WIN, dtype=jnp.int32))
    mixed = mixed_acc.astype(jnp.bfloat16)
    grad_tokens = back_acc.astype(jnp.bfloat16)
    return (mixed, grad_tokens, grad_gate, grad_up, grad_down)
```

```python
import functools

import jax
import jax.numpy as jnp
from jax import lax
from jax.experimental import pallas as pl
from jax.experimental.pallas import tpu as pltpu
from jax.sharding import PartitionSpec as P

QHI = 24
CH = 3
SL = QHI // CH
MESH = pl.DeviceIdType.MESH
F32 = jnp.float32
BF16 = jnp.bfloat16
ROWS = (((0,), (0,)), ((), ()))
COLS = (((1,), (1,)), ((), ()))


def dot(a, b, dims=(((1,), (0,)), ((), ()))):
    return lax.dot_general(a, b, dims, preferred_element_type=F32)


def kernel(
    n_exp, n_z,
    tokens, cot, route, prob, quota, wg_in, wu_in, wd_in,
    mixed, gtok, ggate, gup, gdown,
    wg, wu, wd, send, recv, trash, xs, gs, part, rsr, ag, outb, cbuf,
    wmat, gacc, gdacc, gsend, gdsend, grecv, gdrecv,
    w_loc, w_snd, w_rcv, d_snd, d_rcv, rs_snd, rs_rcv, ag_snd, ag_rcv,
    c_snd, c_rcv, g_snd, g_rcv,
):
    dp = lax.axis_index("dp")
    me = lax.axis_index("expert")
    z = dp // 2
    core = lax.rem(dp, 2)
    par = lax.rem(me, 2)
    n_src = n_exp // 2
    half = n_z // 2
    tok_n, feat = tokens.shape
    hid = wg.shape[1]
    hh = hid // 2
    rows = n_src * SL
    zr = rows // n_z
    lanes = 128

    def dev(e, zz, cc):
        return {"expert": e, "dp": zz * 2 + cc}

    right, left = lax.rem(z + 1, n_z), lax.rem(z + n_z - 1, n_z)

    barrier = pltpu.get_barrier_semaphore()

    def greet(e, zz, cc):
        pl.semaphore_signal(barrier, inc=1, device_id=dev(e, zz, cc), device_id_type=MESH)

    greet(me, right, core)
    greet(me, left, core)

    @pl.loop(0, n_exp)
    def _(t):
        e = lax.rem(me + t, n_exp)

        @pl.when(jnp.logical_or(t > 0, core != par))
        def _():
            greet(e, z, par)

    @pl.loop(0, n_src)
    def _(t):
        greet(2 * t + core, z, 1 - par)

    own = [
        pltpu.make_async_copy(wg_in.at[0], wg.at[pl.ds(core * feat, feat)], w_loc.at[0]),
        pltpu.make_async_copy(wu_in.at[0], wu.at[pl.ds(core * feat, feat)], w_loc.at[1]),
        pltpu.make_async_copy(wd_in.at[0], wd.at[core], w_loc.at[2]),
    ]
    for copy in own:
        copy.start()

    lane = lax.broadcasted_iota(jnp.int32, (tok_n, lanes), 1)
    match = jnp.zeros((tok_n, lanes), F32)
    pe = jnp.zeros((tok_n, lanes), F32)
    for k in range(route.shape[1]):
        hit = route[:, k : k + 1] == lane
        match = jnp.where(hit, 1.0, match)
        pe = jnp.where(hit, prob[:, k : k + 1], pe)
    lower = lax.broadcasted_iota(jnp.int32, (tok_n, tok_n), 1) < lax.broadcasted_iota(
        jnp.int32, (tok_n, tok_n), 0
    )
    before = dot(lower.astype(F32).astype(BF16), match.astype(BF16))
    lane1 = lax.broadcasted_iota(jnp.int32, (1, lanes), 1)
    quotas = jnp.zeros((1, lanes), jnp.int32)
    for e in range(n_exp):
        quotas = jnp.where(lane1 == e, quota[e], quotas)
    eff = jnp.where((match > 0.0) & (before < quotas.astype(F32)), before, 255.0)
    eff_t = eff.T[:n_exp]
    pe_t = pe.T[:n_exp]

    others = par == core
    pl.semaphore_wait(barrier, n_exp + n_src + 2 - others.astype(jnp.int32))

    shared = [
        (wg_in.at[0], wg.at[pl.ds(core * feat, feat)]),
        (wu_in.at[0], wu.at[pl.ds(core * feat, feat)]),
        (wd_in.at[0], wd.at[core]),
    ]

    def weight_copy(i):
        return pltpu.make_async_remote_copy(
            src_ref=shared[i][0], dst_ref=shared[i][1], send_sem=w_snd.at[i], recv_sem=w_rcv.at[i],
            device_id=dev(me, z, 1 - core), device_id_type=MESH,
        )

    slot = lax.broadcasted_iota(jnp.int32, (n_exp, SL, tok_n), 1).astype(F32)
    for c in range(CH):
        hit = eff_t[:, None, :] == slot + float(c * SL)
        pick = jnp.where(hit, 1.0, 0.0).reshape(n_exp * SL, tok_n)
        weight = jnp.where(hit, pe_t[:, None, :], 0.0).reshape(n_exp * SL, tok_n)
        slot_prob = jnp.sum(weight, axis=1, keepdims=True)
        pick = pick.astype(BF16)
        picked = dot(pick, tokens[...]).reshape(n_exp, SL, feat)
        grads = (dot(pick, cot[...]) * slot_prob).reshape(n_exp, SL, feat)
        send[c] = jnp.concatenate([picked, grads], axis=1).astype(BF16)

        @pl.loop(0, n_exp)
        def _(t):
            e = lax.rem(me + t + 1, n_exp)
            there = jnp.logical_or(e != me, core != par)

            @pl.when(there)
            def _():
                pltpu.make_async_remote_copy(
                    src_ref=send.at[c, e], dst_ref=recv.at[c, core, me // 2],
                    send_sem=d_snd.at[c], recv_sem=d_rcv.at[c],
                    device_id=dev(e, z, par), device_id_type=MESH,
                ).start()

            @pl.when(jnp.logical_not(there))
            def _():
                pltpu.make_async_copy(send.at[c, e], recv.at[c, core, me // 2], d_rcv.at[c]).start()
                pltpu.make_async_copy(send.at[c, e], trash.at[0, c], d_snd.at[c]).start()

        if c == 0:
            for i in range(3):
                weight_copy(i).start()

    wide = n_exp * 2 * SL
    spread = (
        lax.broadcasted_iota(jnp.int32, (lanes, wide), 1) // (2 * SL)
        == lax.broadcasted_iota(jnp.int32, (lanes, wide), 0)
    ).astype(F32).astype(BF16)
    eff_x = dot(eff.astype(BF16), spread)
    pe_hi = pe.astype(BF16)
    pe_lo = (pe - pe_hi.astype(F32)).astype(BF16)
    hi_x = dot(pe_hi, spread)
    lo_x = dot(pe_lo, spread)
    place = lax.rem(lax.broadcasted_iota(jnp.int32, (tok_n, wide), 1), 2 * SL)
    for c in range(CH):
        out_hit = eff_x == (place + c * SL).astype(F32)
        out_hit = out_hit & (place < SL)
        back_hit = (eff_x == (place + (c - 1) * SL).astype(F32)) & (place >= SL)
        wmat[c, 0] = jnp.where(out_hit, hi_x, 0.0).astype(BF16)
        wmat[c, 1] = jnp.where(out_hit, lo_x, 0.0).astype(BF16)
        wmat[c, 2] = jnp.where(back_hit, 1.0, 0.0).astype(BF16)

    for copy in own:
        copy.wait()
    for i in range(3):
        weight_copy(i).wait_recv()

    def rs_copy(c, way, step):
        k = half - step
        if way == 0:
            d, to = lax.rem(z + k, n_z), right
        else:
            d, to = lax.rem(z + n_z - k, n_z), left
        src, dst = part.at[c, d], rsr.at[c, way, step]
        if step == 0:
            src, dst = src.at[way], dst.at[way]
        return pltpu.make_async_remote_copy(
            src_ref=src, dst_ref=dst, send_sem=rs_snd.at[c, way, step], recv_sem=rs_rcv.at[c, way, step],
            device_id=dev(me, to, core), device_id_type=MESH,
        )

    def ag_copy(c, way, step):
        if way == 0:
            d, to = lax.rem(z + n_z - step, n_z), right
        else:
            d, to = lax.rem(z + step, n_z), left
        ref = ag.at[c, d]
        if step == half - 1:
            ref = ref.at[way]
        return pltpu.make_async_remote_copy(
            src_ref=ref, dst_ref=ref, send_sem=ag_snd.at[c, way, step], recv_sem=ag_rcv.at[c, way, step],
            device_id=dev(me, to, core), device_id_type=MESH,
        )

    def ag_landed(c, way, step):
        if way == 0:
            d = lax.rem(z + n_z - step - 1, n_z)
        else:
            d = lax.rem(z + step + 1, n_z)
        ref = ag.at[c, d]
        if step == half - 1:
            ref = ref.at[way]
        return pltpu.make_async_copy(ref, ref, ag_rcv.at[c, way, step])

    def rs_landed(c, way, step):
        ref = rsr.at[c, way, step]
        if step == 0:
            ref = ref.at[way]
        return pltpu.make_async_copy(ref, ref, rs_rcv.at[c, way, step])

    def first(c):
        pltpu.make_async_copy(recv.at[c], recv.at[c], d_rcv.at[c]).wait()
        gate = up = back = None
        for b in range(2):
            both = recv[c, b].astype(F32)
            x = both[:, :SL].reshape(rows, feat).astype(BF16)
            g = both[:, SL:].reshape(rows, feat).astype(BF16)
            xs[b, c * rows : (c + 1) * rows] = x
            gs[b, c * rows : (c + 1) * rows] = g
        x = jnp.concatenate([xs[0, c * rows : (c + 1) * rows], xs[1, c * rows : (c + 1) * rows]], axis=1)
        for h in range(2):
            cols = slice(h * hh, (h + 1) * hh)
            gate = dot(x, wg[:, cols]).astype(BF16).reshape(n_z, zr, hh)
            up = dot(x, wu[:, cols]).astype(BF16).reshape(n_z, zr, hh)
            back = dot(gs[0, c * rows : (c + 1) * rows], wd[0, cols], COLS)
            back = back + dot(gs[1, c * rows : (c + 1) * rows], wd[1, cols], COLS)
            back = back.astype(BF16).reshape(n_z, zr, hh)
            part[c, :, h, 0:zr] = gate
            part[c, :, h, zr : 2 * zr] = up
            part[c, :, h, 2 * zr : 3 * zr] = back
        for way in range(2):
            rs_copy(c, way, 0).start()

    def rs_hop(c, step):
        for way in range(2):
            rs_landed(c, way, step - 1).wait()
            k = half - step
            d = lax.rem(z + k, n_z) if way == 0 else lax.rem(z + n_z - k, n_z)
            if step == 1:
                part[c, d, way] = (part[c, d, way].astype(F32) + rsr[c, way, 0, way].astype(F32)).astype(BF16)
            else:
                part[c, d] = (part[c, d].astype(F32) + rsr[c, way, step - 1].astype(F32)).astype(BF16)
            rs_copy(c, way, step).start()

    def middle(c):
        for way in range(2):
            rs_landed(c, way, half - 1).wait()
        total = part[c, z].astype(F32) + rsr[c, 0, half - 1].astype(F32) + rsr[c, 1, half - 1].astype(F32)
        gate, up, back = total[:, 0:zr], total[:, zr : 2 * zr], total[:, 2 * zr :]
        sig = jax.nn.sigmoid(gate)
        act = gate * sig
        hidden = act * up
        grad_pre = back * up * sig * (1.0 + gate * (1.0 - sig))
        grad_up = back * act
        ag[c, z, :, 0:zr] = hidden.astype(BF16)
        ag[c, z, :, zr : 2 * zr] = grad_pre.astype(BF16)
        ag[c, z, :, 2 * zr : 3 * zr] = grad_up.astype(BF16)
        for way in range(2):
            ag_copy(c, way, 0).start()

    def ag_hop(c, step):
        for way in range(2):
            ag_landed(c, way, step - 1).wait()
            ag_copy(c, way, step).start()

    def piece(c, i, h):
        return ag[c, :, h, i * zr : (i + 1) * zr].reshape(rows, hh)

    def last(c):
        for way in range(2):
            ag_landed(c, way, half - 1).wait()
        for b in range(2):
            out = back = None
            for h in range(2):
                cols = slice(h * hh, (h + 1) * hh)
                fs = slice(b * feat, (b + 1) * feat)
                o = dot(piece(c, 0, h), wd[b, cols])
                r = dot(piece(c, 1, h), wg[fs, cols], COLS) + dot(piece(c, 2, h), wu[fs, cols], COLS)
                out = o if out is None else out + o
                back = r if back is None else back + r
            outb[c, b] = jnp.concatenate(
                [out.reshape(n_src, SL, feat), back.reshape(n_src, SL, feat)], axis=1
            ).astype(BF16)

        @pl.loop(0, n_exp)
        def _(t):
            i = lax.rem(me // 2 + t // 2 + 1, n_src)
            b = lax.rem(t, 2)
            j = 2 * i + core
            there = jnp.logical_or(j != me, b != core)

            @pl.when(there)
            def _():
                pltpu.make_async_remote_copy(
                    src_ref=outb.at[c, b, i], dst_ref=cbuf.at[c, me],
                    send_sem=c_snd.at[c], recv_sem=c_rcv.at[c],
                    device_id=dev(j, z, b), device_id_type=MESH,
                ).start()

            @pl.when(jnp.logical_not(there))
            def _():
                pltpu.make_async_copy(outb.at[c, b, i], cbuf.at[c, me], c_rcv.at[c]).start()
                pltpu.make_async_copy(outb.at[c, b, i], trash.at[1, c], c_snd.at[c]).start()

    stages = [first]
    for s in range(1, half):
        stages.append(functools.partial(rs_hop, step=s))
    stages.append(middle)
    for s in range(1, half):
        stages.append(functools.partial(ag_hop, step=s))
    stages.append(last)
    skew = 1
    for t in range(len(stages) + skew * (CH - 1)):
        for c in range(CH):
            s = t - skew * c
            if 0 <= s < len(stages):
                stages[s](c)

    def all_of(i, h):
        return jnp.concatenate([piece(c, i, h) for c in range(CH)], axis=0)

    for h in range(2):
        cols = slice(h * hh, (h + 1) * hh)
        gsend[0, :, cols] = dot(xs[1 - core], all_of(1, h), ROWS).astype(BF16)
        gsend[1, :, cols] = dot(xs[1 - core], all_of(2, h), ROWS).astype(BF16)
        gdsend[cols] = dot(all_of(0, h), gs[1 - core], ROWS).astype(BF16)

    def grad_copy(i):
        src, dst = ((gsend, grecv), (gdsend, gdrecv))[i]
        return pltpu.make_async_remote_copy(
            src_ref=src, dst_ref=dst, send_sem=g_snd.at[i], recv_sem=g_rcv.at[i],
            device_id=dev(me, z, 1 - core), device_id_type=MESH,
        )

    for i in range(2):
        grad_copy(i).start()
    for h in range(2):
        cols = slice(h * hh, (h + 1) * hh)
        gacc[0, :, cols] = dot(xs[core], all_of(1, h), ROWS)
        gacc[1, :, cols] = dot(xs[core], all_of(2, h), ROWS)
        gdacc[cols] = dot(all_of(0, h), gs[core], ROWS)

    for i in range(2):
        grad_copy(i).wait_recv()
    ggate[0] = (gacc[0] + grecv[0].astype(F32)).astype(BF16)
    gup[0] = (gacc[1] + grecv[1].astype(F32)).astype(BF16)
    gdown[0] = (gdacc[...] + gdrecv[...].astype(F32)).astype(BF16)

    mix = grad = None
    for c in range(CH):
        pltpu.make_async_copy(cbuf.at[c], cbuf.at[c], c_rcv.at[c]).wait()
        got = cbuf[c].reshape(wide, feat)
        m = dot(wmat[c, 0], got) + dot(wmat[c, 1], got)
        g = dot(wmat[c, 2], got)
        mix = m if mix is None else mix + m
        grad = g if grad is None else grad + g
    mixed[...] = mix.astype(BF16)
    gtok[...] = grad.astype(BF16)

    for i in range(3):
        weight_copy(i).wait_send()
    for i in range(2):
        grad_copy(i).wait_send()
    for c in range(CH):
        pltpu.make_async_copy(send.at[c], send.at[c], d_snd.at[c]).wait()
        pltpu.make_async_copy(outb.at[c], outb.at[c], c_snd.at[c]).wait()
        for way in range(2):
            for s in range(half):
                rs_copy(c, way, s).wait_send()
                ag_copy(c, way, s).wait_send()


def local(tokens, cotangent, route, prob, quota, w_gate, w_up, w_down):
    n_exp = lax.axis_size("expert")
    n_z = lax.axis_size("dp") // 2
    tok_n, feat = tokens.shape
    hid = w_gate.shape[2]
    half = n_z // 2
    n_src = n_exp // 2
    rows = n_src * SL
    zr = rows // n_z
    hh = hid // 2
    vm = pl.BlockSpec(memory_space=pltpu.VMEM)
    hbm = pl.BlockSpec(memory_space=pl.ANY)
    sm = pl.BlockSpec(memory_space=pltpu.SMEM)
    dma = pltpu.SemaphoreType.DMA
    return pl.pallas_call(
        functools.partial(kernel, n_exp, n_z),
        out_shape=(
            jax.ShapeDtypeStruct((tok_n, feat), BF16),
            jax.ShapeDtypeStruct((tok_n, feat), BF16),
            jax.ShapeDtypeStruct((1, feat, hid), BF16),
            jax.ShapeDtypeStruct((1, feat, hid), BF16),
            jax.ShapeDtypeStruct((1, hid, feat), BF16),
        ),
        in_specs=[vm, vm, vm, vm, sm, hbm, hbm, hbm],
        out_specs=[vm] * 5,
        scratch_shapes=[
            pltpu.VMEM((2 * feat, hid), BF16),
            pltpu.VMEM((2 * feat, hid), BF16),
            pltpu.VMEM((2, hid, feat), BF16),
            pltpu.VMEM((CH, n_exp, 2 * SL, feat), BF16),
            pltpu.VMEM((CH, 2, n_src, 2 * SL, feat), BF16),
            pltpu.VMEM((2, CH, 2 * SL, feat), BF16),
            pltpu.VMEM((2, CH * rows, feat), BF16),
            pltpu.VMEM((2, CH * rows, feat), BF16),
            pltpu.VMEM((CH, n_z, 2, 3 * zr, hh), BF16),
            pltpu.VMEM((CH, 2, half, 2, 3 * zr, hh), BF16),
            pltpu.VMEM((CH, n_z, 2, 3 * zr, hh), BF16),
            pltpu.VMEM((CH, 2, n_src, 2 * SL, feat), BF16),
            pltpu.VMEM((CH, n_exp, 2 * SL, feat), BF16),
            pltpu.VMEM((CH, 3, tok_n, n_exp * 2 * SL), BF16),
            pltpu.VMEM((2, feat, hid), F32),
            pltpu.VMEM((hid, feat), F32),
            pltpu.VMEM((2, feat, hid), BF16),
            pltpu.VMEM((hid, feat), BF16),
            pltpu.VMEM((2, feat, hid), BF16),
            pltpu.VMEM((hid, feat), BF16),
            dma((3,)), dma((3,)), dma((3,)),
            dma((CH,)), dma((CH,)),
            dma((CH, 2, half)), dma((CH, 2, half)),
            dma((CH, 2, half)), dma((CH, 2, half)),
            dma((CH,)), dma((CH,)),
            dma((2,)), dma((2,)),
        ],
        compiler_params=pltpu.CompilerParams(
            collective_id=0, has_side_effects=True, vmem_limit_bytes=56 * 1024 * 1024
        ),
    )(tokens, cotangent, route, prob, quota, w_gate, w_up, w_down)


def solution(mesh):
    placed = (
        P("expert", "dp"),
        P("expert", "dp"),
        P("expert", None),
        P("expert", None),
        P(),
        P("expert", "dp", None),
        P("expert", "dp", None),
        P("expert", None, "dp"),
    )
    return jax.shard_map(
        local,
        mesh=mesh,
        in_specs=placed,
        out_specs=(
            P("expert", "dp"),
            P("expert", "dp"),
            P("expert", "dp", None),
            P("expert", "dp", None),
            P("expert", None, "dp"),
        ),
        check_vma=False,
    )
```

```python
import functools

import jax
import jax.numpy as jnp
from jax import lax
from jax.experimental import pallas as pl
from jax.experimental.pallas import tpu as pltpu
from jax.sharding import PartitionSpec as P

QHI = 24
CH = 3
SL = QHI // CH
MESH = pl.DeviceIdType.MESH
F32 = jnp.float32
BF16 = jnp.bfloat16
ROWS = (((0,), (0,)), ((), ()))
COLS = (((1,), (1,)), ((), ()))


def dot(a, b, dims=(((1,), (0,)), ((), ()))):
    return lax.dot_general(a, b, dims, preferred_element_type=F32)


ARRIVE, BUSY, FLIGHT = 6.5, 2.0, 2.0


def stage_order(count):
    ready, stage, link, order = [ARRIVE * (c + 1) for c in range(CH)], [0] * CH, 0.0, []
    while len(order) < CH * count:
        c = min((c for c in range(CH) if stage[c] < count), key=lambda c: (ready[c], c))
        order.append((c, stage[c]))
        link = max(link, ready[c]) + BUSY
        ready[c] = link + FLIGHT
        stage[c] += 1
    return order


def kernel(
    n_exp, n_z,
    tok_in, cot_in, route, prob, quota, wg_in, wu_in, wd_in,
    mixed, gtok, ggate, gup, gdown,
    tokens, cot,
    wg, wu, wd, send, recv, trash, xs, gs, part, rsr, ag, outb, cbuf,
    wmat, mixacc, gacc, gdacc, agx, xsx, gsx,
    t_loc, w_loc, w_snd, w_rcv, d_snd, d_rcv, rs_snd, rs_rcv, ag_snd, ag_rcv,
    c_snd, c_rcv, x_snd, x_rcv, m_snd, m_rcv,
):
    dp = lax.axis_index("dp")
    me = lax.axis_index("expert")
    z = dp // 2
    core = lax.rem(dp, 2)
    par = lax.rem(me, 2)
    n_src = n_exp // 2
    half = n_z // 2
    tok_n, feat = tokens.shape
    hid = wg.shape[1]
    hh = hid // 2
    rows = n_src * SL
    zr = rows // n_z
    per = zr // SL
    lanes = 128

    def dev(e, zz, cc):
        return {"expert": e, "dp": zz * 2 + cc}

    right, left = lax.rem(z + 1, n_z), lax.rem(z + n_z - 1, n_z)

    loads = [
        pltpu.make_async_copy(tok_in, tokens, t_loc.at[0]),
        pltpu.make_async_copy(cot_in, cot, t_loc.at[1]),
    ]
    for copy in loads:
        copy.start()

    barrier = pltpu.get_barrier_semaphore()

    def greet(e, zz, cc):
        pl.semaphore_signal(barrier, inc=1, device_id=dev(e, zz, cc), device_id_type=MESH)

    greet(me, right, core)
    greet(me, left, core)

    @pl.loop(1, n_exp)
    def _(t):
        greet(lax.rem(me + t, n_exp), z, par)

    @pl.when(core != par)
    def _():
        greet(me, z, par)

    @pl.loop(0, n_src)
    def _(t):
        greet(2 * t + core, z, 1 - par)

    own = [
        pltpu.make_async_copy(wg_in.at[0], wg.at[pl.ds(core * feat, feat)], w_loc.at[0]),
        pltpu.make_async_copy(wu_in.at[0], wu.at[pl.ds(core * feat, feat)], w_loc.at[1]),
        pltpu.make_async_copy(wd_in.at[0], wd.at[core], w_loc.at[2]),
    ]
    for copy in own:
        copy.start()

    mine = lax.broadcasted_iota(jnp.int32, (n_exp, tok_n), 0)
    match = jnp.zeros((n_exp, tok_n), F32)
    pe_t = jnp.zeros((n_exp, tok_n), F32)
    for k in range(route.shape[0]):
        hit = route[k : k + 1] == mine
        match = jnp.where(hit, 1.0, match)
        pe_t = jnp.where(hit, prob[k : k + 1], pe_t)
    earlier = lax.broadcasted_iota(jnp.int32, (tok_n, tok_n), 0) < lax.broadcasted_iota(
        jnp.int32, (tok_n, tok_n), 1
    )
    before = dot(match.astype(BF16), earlier.astype(F32).astype(BF16))
    row1 = lax.broadcasted_iota(jnp.int32, (n_exp, 1), 0)
    quotas = jnp.zeros((n_exp, 1), jnp.int32)
    for e in range(n_exp):
        quotas = jnp.where(row1 == e, quota[e], quotas)
    eff_t = jnp.where((match > 0.0) & (before < quotas.astype(F32)), before, 255.0)
    for copy in loads:
        copy.wait()

    others = par == core
    pl.semaphore_wait(barrier, n_exp + n_src + 2 - others.astype(jnp.int32))

    shared = [
        (wg_in.at[0], wg.at[pl.ds(core * feat, feat)]),
        (wu_in.at[0], wu.at[pl.ds(core * feat, feat)]),
        (wd_in.at[0], wd.at[core]),
    ]

    def weight_copy(i):
        return pltpu.make_async_remote_copy(
            src_ref=shared[i][0], dst_ref=shared[i][1], send_sem=w_snd.at[i], recv_sem=w_rcv.at[i],
            device_id=dev(me, z, 1 - core), device_id_type=MESH,
        )

    slot = lax.broadcasted_iota(jnp.int32, (n_exp, SL, tok_n), 1).astype(F32)
    for c in range(CH):
        hit = eff_t[:, None, :] == slot + float(c * SL)
        pick = jnp.where(hit, 1.0, 0.0).reshape(n_exp * SL, tok_n)
        weight = jnp.where(hit, pe_t[:, None, :], 0.0).reshape(n_exp * SL, tok_n)
        slot_prob = jnp.sum(weight, axis=1, keepdims=True)
        pick = pick.astype(BF16)
        picked = dot(pick, tokens[...]).reshape(n_exp, SL, feat)
        grads = (dot(pick, cot[...]) * slot_prob).reshape(n_exp, SL, feat)
        send[c] = jnp.concatenate([picked, grads], axis=1).astype(BF16)

        def to_expert(e):
            return pltpu.make_async_remote_copy(
                src_ref=send.at[c, e], dst_ref=recv.at[c, core, me // 2],
                send_sem=d_snd.at[c], recv_sem=d_rcv.at[c],
                device_id=dev(e, z, par), device_id_type=MESH,
            )

        @pl.loop(1, n_exp)
        def _(t):
            to_expert(lax.rem(me + t, n_exp)).start()

        @pl.when(core != par)
        def _():
            to_expert(me).start()

        @pl.when(core == par)
        def _():
            pltpu.make_async_copy(send.at[c, me], recv.at[c, core, me // 2], d_rcv.at[c]).start()
            pltpu.make_async_copy(send.at[c, me], trash.at[0, c], d_snd.at[c]).start()

        if c == 0:
            for i in range(3):
                weight_copy(i).start()

    for copy in own:
        copy.wait()
    for i in range(3):
        weight_copy(i).wait_recv()

    wide = n_exp * 2 * SL

    def tables(c):
        fill = jnp.zeros((lanes - n_exp, tok_n), F32)
        eff = jnp.concatenate([eff_t, fill], axis=0).T.astype(BF16)
        pe = jnp.concatenate([pe_t, fill], axis=0).T
        spread = (
            lax.broadcasted_iota(jnp.int32, (lanes, wide), 1) // (2 * SL)
            == lax.broadcasted_iota(jnp.int32, (lanes, wide), 0)
        ).astype(F32).astype(BF16)
        pe_hi = pe.astype(BF16)
        pe_lo = (pe - pe_hi.astype(F32)).astype(BF16)
        eff_x = dot(eff, spread)
        place = lax.rem(lax.broadcasted_iota(jnp.int32, (tok_n, wide), 1), 2 * SL)
        hit = eff_x == (lax.rem(place, SL) + c * SL).astype(F32)
        out_hit = hit & (place < SL)
        wmat[c, 0] = jnp.where(out_hit, dot(pe_hi, spread), 0.0).astype(BF16)
        wmat[c, 1] = jnp.where(out_hit, dot(pe_lo, spread), 0.0).astype(BF16)
        wmat[c, 2] = jnp.where(hit & (place >= SL), 1.0, 0.0).astype(BF16)

    def away(way, k):
        return lax.rem(z + k, n_z) if way == 0 else lax.rem(z + n_z - k, n_z)

    def longest(h, way):
        return half if way == h else half - 1

    def rs_copy(c, h, way, k):
        return pltpu.make_async_remote_copy(
            src_ref=part.at[c, away(way, k), h], dst_ref=rsr.at[c, h, way, k - 1],
            send_sem=rs_snd.at[c, h, way, k - 1], recv_sem=rs_rcv.at[c, h, way, k - 1],
            device_id=dev(me, (right, left)[way], core), device_id_type=MESH,
        )

    def rs_landed(c, h, way, k):
        ref = rsr.at[c, h, way, k - 1]
        return pltpu.make_async_copy(ref, ref, rs_rcv.at[c, h, way, k - 1])

    def ag_copy(c, h, way, k):
        ref = ag.at[c, away(1 - way, k), h]
        return pltpu.make_async_remote_copy(
            src_ref=ref, dst_ref=ref, send_sem=ag_snd.at[c, h, way, k], recv_sem=ag_rcv.at[c, h, way, k],
            device_id=dev(me, (right, left)[way], core), device_id_type=MESH,
        )

    def ag_landed(c, h, way, k):
        ref = ag.at[c, away(1 - way, k + 1), h]
        return pltpu.make_async_copy(ref, ref, ag_rcv.at[c, h, way, k])

    def first(c):
        pltpu.make_async_copy(recv.at[c], recv.at[c], d_rcv.at[c]).wait()
        gate = up = back = None
        for b in range(2):
            both = recv[c, b].astype(F32)
            x = both[:, :SL].reshape(rows, feat).astype(BF16)
            g = both[:, SL:].reshape(rows, feat).astype(BF16)
            xs[b, c * rows : (c + 1) * rows] = x
            gs[b, c * rows : (c + 1) * rows] = g
        x = jnp.concatenate([xs[0, c * rows : (c + 1) * rows], xs[1, c * rows : (c + 1) * rows]], axis=1)
        for h in range(2):
            cols = slice(h * hh, (h + 1) * hh)
            gate = dot(x, wg[:, cols]).astype(BF16).reshape(n_z, zr, hh)
            up = dot(x, wu[:, cols]).astype(BF16).reshape(n_z, zr, hh)
            back = dot(gs[0, c * rows : (c + 1) * rows], wd[0, cols], COLS)
            back = back + dot(gs[1, c * rows : (c + 1) * rows], wd[1, cols], COLS)
            back = back.astype(BF16).reshape(n_z, zr, hh)
            part[c, :, h, 0:zr] = gate
            part[c, :, h, zr : 2 * zr] = up
            part[c, :, h, 2 * zr : 3 * zr] = back
        for h in range(2):
            for way in (h, 1 - h):
                rs_copy(c, h, way, longest(h, way)).start()

        for i in range(2):
            x_copy(c, i).start()

    def to_sibling(src, dst, snd, rcv):
        return pltpu.make_async_remote_copy(
            src_ref=src, dst_ref=dst, send_sem=snd, recv_sem=rcv,
            device_id=dev(me, z, 1 - core), device_id_type=MESH,
        )

    def x_copy(c, i):
        src, dst = ((xs, xsx), (gs, gsx))[i]
        part_rows = pl.ds(c * rows, rows)
        return to_sibling(src.at[1 - core, part_rows], dst.at[part_rows], x_snd.at[c, i], x_rcv.at[c, i])

    def block_at(p):
        return away(p % 2, (p + 1) // 2)

    def m_copy(c, p):
        d = block_at(p)
        return to_sibling(ag.at[c, d], agx.at[c, d], m_snd.at[c, p], m_rcv.at[c, p])

    def rs_hop(c, step):
        for h in range(2):
            for way in (h, 1 - h):
                k = longest(h, way) - step
                if k >= 1:
                    rs_landed(c, h, way, k + 1).wait()
                    d = away(way, k)
                    part[c, d, h] = (part[c, d, h].astype(F32) + rsr[c, h, way, k].astype(F32)).astype(BF16)
                    rs_copy(c, h, way, k).start()

    def middle(c):
        for h in range(2):
            for way in (1 - h, h):
                rs_landed(c, h, way, 1).wait()
            total = part[c, z, h].astype(F32) + rsr[c, h, 0, 0].astype(F32) + rsr[c, h, 1, 0].astype(F32)
            gate, up, back = total[0:zr], total[zr : 2 * zr], total[2 * zr :]
            sig = jax.nn.sigmoid(gate)
            act = gate * sig
            ag[c, z, h, 0:zr] = (act * up).astype(BF16)
            ag[c, z, h, zr : 2 * zr] = (back * up * sig * (1.0 + gate * (1.0 - sig))).astype(BF16)
            ag[c, z, h, 2 * zr : 3 * zr] = (back * act).astype(BF16)
            for way in (h, 1 - h):
                ag_copy(c, h, way, 0).start()
        stream(c, [0])

    def ag_hop(c, step):
        for h in range(2):
            for way in (h, 1 - h):
                if step < longest(h, way):
                    ag_landed(c, h, way, step - 1).wait()
                    ag_copy(c, h, way, step).start()
                else:
                    ag_landed(c, h, way, step - 1).wait()
        stream(c, [2 * step - 1, 2 * step])

    def piece(c, i, h, held=ag):
        return held[c, :, h, i * zr : (i + 1) * zr].reshape(rows, hh)

    def to_token(c, i, b):
        return pltpu.make_async_remote_copy(
            src_ref=outb.at[c, b, i], dst_ref=cbuf.at[c, me],
            send_sem=c_snd.at[c], recv_sem=c_rcv.at[c],
            device_id=dev(2 * i + core, z, b), device_id_type=MESH,
        )

    def to_self(c):
        pltpu.make_async_copy(outb.at[c, core, me // 2], cbuf.at[c, me], c_rcv.at[c]).start()
        pltpu.make_async_copy(outb.at[c, core, me // 2], trash.at[1, c], c_snd.at[c]).start()

    def products(get, b):
        out = back = None
        for h in range(2):
            cols = slice(h * hh, (h + 1) * hh)
            fs = slice(b * feat, (b + 1) * feat)
            o = dot(get(0, h), wd[b, cols])
            r = dot(get(1, h), wg[fs, cols], COLS) + dot(get(2, h), wu[fs, cols], COLS)
            out = o if out is None else out + o
            back = r if back is None else back + r
        both = [v.reshape(v.shape[0] // SL, SL, feat) for v in (out, back)]
        return jnp.concatenate(both, axis=1).astype(BF16)

    def stream(c, places):
        ds = [block_at(p) for p in places]
        for p in places:
            m_copy(c, p).start()

        def get(i, h):
            return jnp.concatenate([ag[c, d, h, i * zr : (i + 1) * zr] for d in ds], axis=0)

        for b in range(2):
            both = products(get, b)
            for q, d in enumerate(ds):
                for r in range(per):
                    outb[c, b, d * per + r] = both[q * per + r]
        for d in ds:
            for r in range(per):
                i = d * per + r
                mine_too = (par == core) & (i == me // 2)
                for b in range(2):
                    here = mine_too & (core == b)

                    @pl.when(jnp.logical_not(here))
                    def _():
                        to_token(c, i, b).start()

                    @pl.when(here)
                    def _():
                        to_self(c)

    def last(c):
        for h in range(2):
            ag_landed(c, h, h, half - 1).wait()
        stream(c, [n_z - 1])

    def weight_grads(c):
        for i in range(2):
            x_copy(c, i).wait_recv()
        for p in range(n_z):
            m_copy(c, p).wait_recv()
        part_rows = slice(c * rows, (c + 1) * rows)
        x = jnp.concatenate([xs[core, part_rows], xsx[part_rows]], axis=0)
        g = jnp.concatenate([gs[core, part_rows], gsx[part_rows]], axis=0)
        for h in range(2):
            cols = slice(h * hh, (h + 1) * hh)
            hidden, pre, up = (
                jnp.concatenate([piece(c, i, h), piece(c, i, h, agx)], axis=0) for i in range(3)
            )
            sums = [dot(x, pre, ROWS), dot(x, up, ROWS), dot(hidden, g, ROWS)]
            refs = [gacc.at[0, :, cols], gacc.at[1, :, cols], gdacc.at[cols]]
            outs = [ggate.at[0, :, cols], gup.at[0, :, cols], gdown.at[0, cols]]
            for total, ref, out in zip(sums, refs, outs):
                if c > 0:
                    total = total + ref[...]
                if c < CH - 1:
                    ref[...] = total
                else:
                    out[...] = total.astype(BF16)

    def mix(c):
        pltpu.make_async_copy(cbuf.at[c], cbuf.at[c], c_rcv.at[c]).wait()
        got = cbuf[c].reshape(wide, feat)
        m = dot(wmat[c, 0], got) + dot(wmat[c, 1], got)
        g = dot(wmat[c, 2], got)
        if c > 0:
            m, g = m + mixacc[0], g + mixacc[1]
        if c < CH - 1:
            mixacc[0], mixacc[1] = m, g
        else:
            mixed[...], gtok[...] = m.astype(BF16), g.astype(BF16)

    stages = [first]
    for s in range(1, half):
        stages.append(functools.partial(rs_hop, step=s))
    stages.append(middle)
    for s in range(1, half):
        stages.append(functools.partial(ag_hop, step=s))
    stages.append(last)
    order = stage_order(len(stages))
    for c, stage in order:
        stages[stage](c)
        if c == 0 and 2 <= stage < 2 + CH:
            tables(stage - 2)
        if (c, stage) == (CH - 1, len(stages) - 2):
            weight_grads(0)
            mix(0)
            weight_grads(1)
    mix(1)
    weight_grads(2)
    mix(2)

    for i in range(3):
        weight_copy(i).wait_send()
    for c in range(CH):
        pltpu.make_async_copy(send.at[c], send.at[c], d_snd.at[c]).wait()
        pltpu.make_async_copy(outb.at[c], outb.at[c], c_snd.at[c]).wait()
        for i in range(2):
            x_copy(c, i).wait_send()
        for p in range(n_z):
            m_copy(c, p).wait_send()
        for h in range(2):
            for way in range(2):
                for k in range(longest(h, way)):
                    rs_copy(c, h, way, k + 1).wait_send()
                    ag_copy(c, h, way, k).wait_send()

def finish(*refs):
    ins, outs, sem = refs[:5], refs[5:10], refs[10]
    copies = [pltpu.make_async_copy(src, dst, sem.at[i]) for i, (src, dst) in enumerate(zip(ins, outs))]
    for copy in copies:
        copy.start()
    for copy in copies:
        copy.wait()


def local(tokens, cotangent, route, prob, quota, w_gate, w_up, w_down):
    n_exp = lax.axis_size("expert")
    n_z = lax.axis_size("dp") // 2
    tok_n, feat = tokens.shape
    hid = w_gate.shape[2]
    half = n_z // 2
    n_src = n_exp // 2
    rows = n_src * SL
    zr = rows // n_z
    hh = hid // 2
    vm = pl.BlockSpec(memory_space=pltpu.VMEM)
    hbm = pl.BlockSpec(memory_space=pltpu.HBM)
    sm = pl.BlockSpec(memory_space=pltpu.SMEM)
    dma = pltpu.SemaphoreType.DMA
    shapes = (
        jax.ShapeDtypeStruct((tok_n, feat), BF16),
        jax.ShapeDtypeStruct((tok_n, feat), BF16),
        jax.ShapeDtypeStruct((1, feat, hid), BF16),
        jax.ShapeDtypeStruct((1, feat, hid), BF16),
        jax.ShapeDtypeStruct((1, hid, feat), BF16),
    )
    outs = pl.pallas_call(
        functools.partial(kernel, n_exp, n_z),
        out_shape=tuple(pltpu.VMEM(s.shape, s.dtype) for s in shapes),
        in_specs=[hbm, hbm, vm, vm, sm, hbm, hbm, hbm],
        out_specs=[vm] * 5,
        scratch_shapes=[
            pltpu.VMEM((tok_n, feat), BF16),
            pltpu.VMEM((tok_n, feat), BF16),
            pltpu.VMEM((2 * feat, hid), BF16),
            pltpu.VMEM((2 * feat, hid), BF16),
            pltpu.VMEM((2, hid, feat), BF16),
            pltpu.VMEM((CH, n_exp, 2 * SL, feat), BF16),
            pltpu.VMEM((CH, 2, n_src, 2 * SL, feat), BF16),
            pltpu.VMEM((2, CH, 2 * SL, feat), BF16),
            pltpu.VMEM((2, CH * rows, feat), BF16),
            pltpu.VMEM((2, CH * rows, feat), BF16),
            pltpu.VMEM((CH, n_z, 2, 3 * zr, hh), BF16),
            pltpu.VMEM((CH, 2, 2, half, 3 * zr, hh), BF16),
            pltpu.VMEM((CH, n_z, 2, 3 * zr, hh), BF16),
            pltpu.VMEM((CH, 2, n_src, 2 * SL, feat), BF16),
            pltpu.VMEM((CH, n_exp, 2 * SL, feat), BF16),
            pltpu.VMEM((CH, 3, tok_n, n_exp * 2 * SL), BF16),
            pltpu.VMEM((2, tok_n, feat), F32),
            pltpu.VMEM((2, feat, hid), F32),
            pltpu.VMEM((hid, feat), F32),
            pltpu.VMEM((CH, n_z, 2, 3 * zr, hh), BF16),
            pltpu.VMEM((CH * rows, feat), BF16),
            pltpu.VMEM((CH * rows, feat), BF16),
            dma((2,)),
            dma((3,)), dma((3,)), dma((3,)),
            dma((CH,)), dma((CH,)),
            dma((CH, 2, 2, half)), dma((CH, 2, 2, half)),
            dma((CH, 2, 2, half)), dma((CH, 2, 2, half)),
            dma((CH,)), dma((CH,)),
            dma((CH, 2)), dma((CH, 2)),
            dma((CH, n_z)), dma((CH, n_z)),
        ],
        compiler_params=pltpu.CompilerParams(
            collective_id=0, has_side_effects=True, vmem_limit_bytes=63000 * 1024
        ),
    )(tokens, cotangent, route.T, prob.T, quota, w_gate, w_up, w_down)
    return pl.pallas_call(
        finish,
        out_shape=shapes,
        in_specs=[vm] * 5,
        out_specs=[hbm] * 5,
        scratch_shapes=[dma((5,))],
        compiler_params=pltpu.CompilerParams(vmem_limit_bytes=8 * 1024 * 1024),
    )(*outs)


def solution(mesh):
    placed = (
        P("expert", "dp"),
        P("expert", "dp"),
        P("expert", None),
        P("expert", None),
        P(),
        P("expert", "dp", None),
        P("expert", "dp", None),
        P("expert", None, "dp"),
    )
    return jax.shard_map(
        local,
        mesh=mesh,
        in_specs=placed,
        out_specs=(
            P("expert", "dp"),
            P("expert", "dp"),
            P("expert", "dp", None),
            P("expert", "dp", None),
            P("expert", None, "dp"),
        ),
        check_vma=False,
    )
```

```python
import functools

import jax
import jax.numpy as jnp
from jax import lax
from jax.experimental import pallas as pl
from jax.experimental.pallas import tpu as pltpu
from jax.sharding import PartitionSpec as P

QHI = 24
CH = 3
SL = QHI // CH
MESH = pl.DeviceIdType.MESH
F32 = jnp.float32
BF16 = jnp.bfloat16
ROWS = (((0,), (0,)), ((), ()))
COLS = (((1,), (1,)), ((), ()))


def dot(a, b, dims=(((1,), (0,)), ((), ()))):
    return lax.dot_general(a, b, dims, preferred_element_type=F32)


ARRIVE, BUSY, FLIGHT, LAG = 6.5, 2.0, 2.0, 3


def stage_order(count):
    ready, stage, link, order = [ARRIVE * (c + 1) for c in range(CH)], [0] * CH, 0.0, []
    while len(order) < CH * count:
        c = min((c for c in range(CH) if stage[c] < count), key=lambda c: (ready[c], c))
        order.append((c, stage[c]))
        link = max(link, ready[c]) + BUSY
        ready[c] = link + FLIGHT
        stage[c] += 1
    return order


def kernel(
    n_exp, n_z,
    tok_in, cot_in, route, prob, quota, wg_in, wu_in, wd_in,
    mixed, gtok, ggate, gup, gdown,
    tokens, cot,
    wg, wu, wd, send, recv, trash, xs, gs, part, rsr, ag, outb, cbuf,
    wmat, mixacc, gacc, gdacc, agx, xsx, gsx,
    t_loc, w_loc, w_snd, w_rcv, d_snd, d_rcv, rs_snd, rs_rcv, ag_snd, ag_rcv,
    c_snd, c_rcv, x_snd, x_rcv, m_snd, m_rcv,
):
    dp = lax.axis_index("dp")
    me = lax.axis_index("expert")
    z = dp // 2
    core = lax.rem(dp, 2)
    par = lax.rem(me, 2)
    n_src = n_exp // 2
    half = n_z // 2
    tok_n, feat = tokens.shape
    hid = wg.shape[1]
    hh = hid // 2
    rows = n_src * SL
    zr = rows // n_z
    per = zr // SL
    lanes = 128

    def dev(e, zz, cc):
        return {"expert": e, "dp": zz * 2 + cc}

    right, left = lax.rem(z + 1, n_z), lax.rem(z + n_z - 1, n_z)

    loads = [
        pltpu.make_async_copy(tok_in, tokens, t_loc.at[0]),
        pltpu.make_async_copy(cot_in, cot, t_loc.at[1]),
    ]
    for copy in loads:
        copy.start()

    barrier = pltpu.get_barrier_semaphore()

    def greet(e, zz, cc):
        pl.semaphore_signal(barrier, inc=1, device_id=dev(e, zz, cc), device_id_type=MESH)

    greet(me, right, core)
    greet(me, left, core)

    @pl.loop(1, n_exp)
    def _(t):
        greet(lax.rem(me + t, n_exp), z, par)

    @pl.when(core != par)
    def _():
        greet(me, z, par)

    @pl.loop(0, n_src)
    def _(t):
        greet(2 * t + core, z, 1 - par)

    own = [
        pltpu.make_async_copy(wg_in.at[0], wg.at[pl.ds(core * feat, feat)], w_loc.at[0]),
        pltpu.make_async_copy(wu_in.at[0], wu.at[pl.ds(core * feat, feat)], w_loc.at[1]),
        pltpu.make_async_copy(wd_in.at[0], wd.at[core], w_loc.at[2]),
    ]
    for copy in own:
        copy.start()

    mine = lax.broadcasted_iota(jnp.int32, (n_exp, tok_n), 0)
    match = jnp.zeros((n_exp, tok_n), F32)
    pe_t = jnp.zeros((n_exp, tok_n), F32)
    for k in range(route.shape[0]):
        hit = route[k : k + 1] == mine
        match = jnp.where(hit, 1.0, match)
        pe_t = jnp.where(hit, prob[k : k + 1], pe_t)
    earlier = lax.broadcasted_iota(jnp.int32, (tok_n, tok_n), 0) < lax.broadcasted_iota(
        jnp.int32, (tok_n, tok_n), 1
    )
    before = dot(match.astype(BF16), earlier.astype(F32).astype(BF16))
    row1 = lax.broadcasted_iota(jnp.int32, (n_exp, 1), 0)
    quotas = jnp.zeros((n_exp, 1), jnp.int32)
    for e in range(n_exp):
        quotas = jnp.where(row1 == e, quota[e], quotas)
    eff_t = jnp.where((match > 0.0) & (before < quotas.astype(F32)), before, 255.0)
    for copy in loads:
        copy.wait()

    shared = [
        (wg_in.at[0], wg.at[pl.ds(core * feat, feat)]),
        (wu_in.at[0], wu.at[pl.ds(core * feat, feat)]),
        (wd_in.at[0], wd.at[core]),
    ]

    def weight_copy(i):
        return pltpu.make_async_remote_copy(
            src_ref=shared[i][0], dst_ref=shared[i][1], send_sem=w_snd.at[i], recv_sem=w_rcv.at[i],
            device_id=dev(me, z, 1 - core), device_id_type=MESH,
        )

    slot = lax.broadcasted_iota(jnp.int32, (n_exp, SL, tok_n), 1).astype(F32)

    def fill(c):
        hit = eff_t[:, None, :] == slot + float(c * SL)
        pick = jnp.where(hit, 1.0, 0.0).reshape(n_exp * SL, tok_n)
        weight = jnp.where(hit, pe_t[:, None, :], 0.0).reshape(n_exp * SL, tok_n)
        slot_prob = jnp.sum(weight, axis=1, keepdims=True)
        pick = pick.astype(BF16)
        picked = dot(pick, tokens[...]).reshape(n_exp, SL, feat)
        grads = (dot(pick, cot[...]) * slot_prob).reshape(n_exp, SL, feat)
        send[c] = jnp.concatenate([picked, grads], axis=1).astype(BF16)

    def dispatch(c):
        def to_expert(e):
            return pltpu.make_async_remote_copy(
                src_ref=send.at[c, e], dst_ref=recv.at[c, core, me // 2],
                send_sem=d_snd.at[c], recv_sem=d_rcv.at[c],
                device_id=dev(e, z, par), device_id_type=MESH,
            )

        @pl.loop(1, n_exp)
        def _(t):
            to_expert(lax.rem(me + t, n_exp)).start()

        @pl.when(core != par)
        def _():
            to_expert(me).start()

        @pl.when(core == par)
        def _():
            pltpu.make_async_copy(send.at[c, me], recv.at[c, core, me // 2], d_rcv.at[c]).start()
            pltpu.make_async_copy(send.at[c, me], trash.at[0, c], d_snd.at[c]).start()

    fill(0)
    others = par == core
    pl.semaphore_wait(barrier, n_exp + n_src + 2 - others.astype(jnp.int32))
    dispatch(0)
    for i in range(3):
        weight_copy(i).start()
    for c in range(1, CH):
        fill(c)
        dispatch(c)
    for copy in own:
        copy.wait()
    for i in range(3):
        weight_copy(i).wait_recv()

    wide = n_exp * 2 * SL

    def tables(c):
        fill = jnp.zeros((lanes - n_exp, tok_n), F32)
        eff = jnp.concatenate([eff_t, fill], axis=0).T.astype(BF16)
        pe = jnp.concatenate([pe_t, fill], axis=0).T
        spread = (
            lax.broadcasted_iota(jnp.int32, (lanes, wide), 1) // (2 * SL)
            == lax.broadcasted_iota(jnp.int32, (lanes, wide), 0)
        ).astype(F32).astype(BF16)
        pe_hi = pe.astype(BF16)
        pe_lo = (pe - pe_hi.astype(F32)).astype(BF16)
        eff_x = dot(eff, spread)
        place = lax.rem(lax.broadcasted_iota(jnp.int32, (tok_n, wide), 1), 2 * SL)
        hit = eff_x == (lax.rem(place, SL) + c * SL).astype(F32)
        out_hit = hit & (place < SL)
        wmat[c, 0] = jnp.where(out_hit, dot(pe_hi, spread), 0.0).astype(BF16)
        wmat[c, 1] = jnp.where(out_hit, dot(pe_lo, spread), 0.0).astype(BF16)
        wmat[c, 2] = jnp.where(hit & (place >= SL), 1.0, 0.0).astype(BF16)

    def away(way, k):
        return lax.rem(z + k, n_z) if way == 0 else lax.rem(z + n_z - k, n_z)

    def longest(h, way):
        return half if way == h else half - 1

    def rs_copy(c, h, way, k):
        return pltpu.make_async_remote_copy(
            src_ref=part.at[c, away(way, k), h], dst_ref=rsr.at[c, h, way, k - 1],
            send_sem=rs_snd.at[c], recv_sem=rs_rcv.at[c, h, way, k - 1],
            device_id=dev(me, (right, left)[way], core), device_id_type=MESH,
        )

    def rs_landed(c, h, way, k):
        ref = rsr.at[c, h, way, k - 1]
        return pltpu.make_async_copy(ref, ref, rs_rcv.at[c, h, way, k - 1])

    def ag_copy(c, h, way, k):
        ref = ag.at[c, away(1 - way, k), h]
        return pltpu.make_async_remote_copy(
            src_ref=ref, dst_ref=ref, send_sem=ag_snd.at[c], recv_sem=ag_rcv.at[c, h, way, k],
            device_id=dev(me, (right, left)[way], core), device_id_type=MESH,
        )

    def ag_landed(c, h, way, k):
        ref = ag.at[c, away(1 - way, k + 1), h]
        return pltpu.make_async_copy(ref, ref, ag_rcv.at[c, h, way, k])

    def first(c):
        pltpu.make_async_copy(recv.at[c], recv.at[c], d_rcv.at[c]).wait()
        gate = up = back = None
        for b in range(2):
            both = recv[c, b].astype(F32)
            x = both[:, :SL].reshape(rows, feat).astype(BF16)
            g = both[:, SL:].reshape(rows, feat).astype(BF16)
            xs[b, c * rows : (c + 1) * rows] = x
            gs[b, c * rows : (c + 1) * rows] = g
        x = jnp.concatenate([xs[0, c * rows : (c + 1) * rows], xs[1, c * rows : (c + 1) * rows]], axis=1)
        for h in range(2):
            cols = slice(h * hh, (h + 1) * hh)
            gate = dot(x, wg[:, cols]).astype(BF16).reshape(n_z, zr, hh)
            up = dot(x, wu[:, cols]).astype(BF16).reshape(n_z, zr, hh)
            back = dot(gs[0, c * rows : (c + 1) * rows], wd[0, cols], COLS)
            back = back + dot(gs[1, c * rows : (c + 1) * rows], wd[1, cols], COLS)
            back = back.astype(BF16).reshape(n_z, zr, hh)
            part[c, :, h, 0:zr] = gate
            part[c, :, h, zr : 2 * zr] = up
            part[c, :, h, 2 * zr : 3 * zr] = back
        for h in range(2):
            for way in (h, 1 - h):
                rs_copy(c, h, way, longest(h, way)).start()
        for i in range(2):
            x_copy(c, i).start()

    def to_sibling(src, dst, snd, rcv):
        return pltpu.make_async_remote_copy(
            src_ref=src, dst_ref=dst, send_sem=snd, recv_sem=rcv,
            device_id=dev(me, z, 1 - core), device_id_type=MESH,
        )

    def x_copy(c, i):
        src, dst = ((xs, xsx), (gs, gsx))[i]
        part_rows = pl.ds(c * rows, rows)
        return to_sibling(src.at[1 - core, part_rows], dst.at[part_rows], x_snd.at[c, i], x_rcv.at[c, i])

    def block_at(p):
        return away(p % 2, (p + 1) // 2)

    def m_copy(c, p):
        d = block_at(p)
        return to_sibling(ag.at[c, d], agx.at[c, d], m_snd.at[c], m_rcv.at[c])

    def rs_hop(c, step):
        for h in range(2):
            for way in (h, 1 - h):
                k = longest(h, way) - step
                if k >= 1:
                    rs_landed(c, h, way, k + 1).wait()
                    d = away(way, k)
                    part[c, d, h] = (part[c, d, h].astype(F32) + rsr[c, h, way, k].astype(F32)).astype(BF16)
                    rs_copy(c, h, way, k).start()

    def middle(c):
        for h in range(2):
            for way in (1 - h, h):
                rs_landed(c, h, way, 1).wait()
            total = part[c, z, h].astype(F32) + rsr[c, h, 0, 0].astype(F32) + rsr[c, h, 1, 0].astype(F32)
            gate, up, back = total[0:zr], total[zr : 2 * zr], total[2 * zr :]
            sig = jax.nn.sigmoid(gate)
            act = gate * sig
            ag[c, z, h, 0:zr] = (act * up).astype(BF16)
            ag[c, z, h, zr : 2 * zr] = (back * up * sig * (1.0 + gate * (1.0 - sig))).astype(BF16)
            ag[c, z, h, 2 * zr : 3 * zr] = (back * act).astype(BF16)
            for way in (h, 1 - h):
                ag_copy(c, h, way, 0).start()
        stream(c, [0])

    def ag_hop(c, step):
        for h in range(2):
            for way in (h, 1 - h):
                if step < longest(h, way):
                    ag_landed(c, h, way, step - 1).wait()
                    ag_copy(c, h, way, step).start()
                else:
                    ag_landed(c, h, way, step - 1).wait()
        stream(c, [2 * step - 1, 2 * step])

    def piece(c, i, h, held=ag):
        return held[c, :, h, i * zr : (i + 1) * zr].reshape(rows, hh)

    def to_token(c, i, b):
        return pltpu.make_async_remote_copy(
            src_ref=outb.at[c, b, i], dst_ref=cbuf.at[c, me],
            send_sem=c_snd.at[c], recv_sem=c_rcv.at[c],
            device_id=dev(2 * i + core, z, b), device_id_type=MESH,
        )

    def to_self(c):
        pltpu.make_async_copy(outb.at[c, core, me // 2], cbuf.at[c, me], c_rcv.at[c]).start()
        pltpu.make_async_copy(outb.at[c, core, me // 2], trash.at[1, c], c_snd.at[c]).start()

    def products(get, b):
        out = back = None
        for h in range(2):
            cols = slice(h * hh, (h + 1) * hh)
            fs = slice(b * feat, (b + 1) * feat)
            o = dot(get(0, h), wd[b, cols])
            r = dot(get(1, h), wg[fs, cols], COLS) + dot(get(2, h), wu[fs, cols], COLS)
            out = o if out is None else out + o
            back = r if back is None else back + r
        both = [v.reshape(v.shape[0] // SL, SL, feat) for v in (out, back)]
        return jnp.concatenate(both, axis=1).astype(BF16)

    def stream(c, places):
        ds = [block_at(p) for p in places]
        for p in places:
            m_copy(c, p).start()

        def get(i, h):
            return jnp.concatenate([ag[c, d, h, i * zr : (i + 1) * zr] for d in ds], axis=0)

        for b in range(2):
            both = products(get, b)
            for q, d in enumerate(ds):
                for r in range(per):
                    outb[c, b, d * per + r] = both[q * per + r]
        for d in ds:
            for r in range(per):
                i = d * per + r
                mine_too = (par == core) & (i == me // 2)
                for b in range(2):
                    here = mine_too & (core == b)

                    @pl.when(jnp.logical_not(here))
                    def _():
                        to_token(c, i, b).start()

                    @pl.when(here)
                    def _():
                        to_self(c)

    def last(c):
        for h in range(2):
            ag_landed(c, h, h, half - 1).wait()
        stream(c, [n_z - 1])

    def weight_grads(c):
        for i in range(2):
            x_copy(c, i).wait_recv()
        pltpu.make_async_copy(agx.at[c], agx.at[c], m_rcv.at[c]).wait()
        part_rows = slice(c * rows, (c + 1) * rows)
        x = jnp.concatenate([xs[core, part_rows], xsx[part_rows]], axis=0)
        g = jnp.concatenate([gs[core, part_rows], gsx[part_rows]], axis=0)
        for h in range(2):
            cols = slice(h * hh, (h + 1) * hh)
            hidden, pre, up = (
                jnp.concatenate([piece(c, i, h), piece(c, i, h, agx)], axis=0) for i in range(3)
            )
            sums = [dot(x, pre, ROWS), dot(x, up, ROWS), dot(hidden, g, ROWS)]
            refs = [gacc.at[0, :, cols], gacc.at[1, :, cols], gdacc.at[cols]]
            outs = [ggate.at[0, :, cols], gup.at[0, :, cols], gdown.at[0, cols]]
            for total, ref, out in zip(sums, refs, outs):
                if c > 0:
                    total = total + ref[...]
                if c < CH - 1:
                    ref[...] = total
                else:
                    out[...] = total.astype(BF16)

    def sent(c):
        for ref, sem in (
            (send.at[c], d_snd), (outb.at[c], c_snd), (ag.at[c], m_snd),
            (part.at[c, 0 : n_z - 1], rs_snd), (ag.at[c, 0 : n_z - 1], ag_snd),
        ):
            pltpu.make_async_copy(ref, ref, sem.at[c]).wait()
        for i in range(2):
            x_copy(c, i).wait_send()

    def mix(c):
        pltpu.make_async_copy(cbuf.at[c], cbuf.at[c], c_rcv.at[c]).wait()
        got = cbuf[c].reshape(wide, feat)
        m = dot(wmat[c, 0], got) + dot(wmat[c, 1], got)
        g = dot(wmat[c, 2], got)
        if c > 0:
            m, g = m + mixacc[0], g + mixacc[1]
        if c < CH - 1:
            mixacc[0], mixacc[1] = m, g
        else:
            mixed[...], gtok[...] = m.astype(BF16), g.astype(BF16)

    stages = [first]
    for s in range(1, half):
        stages.append(functools.partial(rs_hop, step=s))
    stages.append(middle)
    for s in range(1, half):
        stages.append(functools.partial(ag_hop, step=s))
    stages.append(last)
    order = stage_order(len(stages))
    place = {(c, stage): n for n, (c, stage) in enumerate(order)}
    after = [[] for _ in order]
    for c in range(CH):
        over = place[(c, len(stages) - 1)]
        after[min(over + 1, len(order) - 1)].append(functools.partial(weight_grads, c))
        after[min(over + LAG, len(order) - 1)].append(functools.partial(mix, c))
        after[place[(0, 2 + c)]].append(functools.partial(tables, c))
    for n, (c, stage) in enumerate(order):
        stages[stage](c)
        for task in after[n]:
            task()

    for c in range(CH):
        sent(c)
    for i in range(3):
        weight_copy(i).wait_send()


def finish(*refs):
    ins, outs, sem = refs[:5], refs[5:10], refs[10]
    copies = [pltpu.make_async_copy(src, dst, sem.at[i]) for i, (src, dst) in enumerate(zip(ins, outs))]
    for copy in copies:
        copy.start()
    for copy in copies:
        copy.wait()


def local(tokens, cotangent, route, prob, quota, w_gate, w_up, w_down):
    n_exp = lax.axis_size("expert")
    n_z = lax.axis_size("dp") // 2
    tok_n, feat = tokens.shape
    hid = w_gate.shape[2]
    half = n_z // 2
    n_src = n_exp // 2
    rows = n_src * SL
    zr = rows // n_z
    hh = hid // 2
    vm = pl.BlockSpec(memory_space=pltpu.VMEM)
    hbm = pl.BlockSpec(memory_space=pltpu.HBM)
    sm = pl.BlockSpec(memory_space=pltpu.SMEM)
    dma = pltpu.SemaphoreType.DMA
    shapes = (
        jax.ShapeDtypeStruct((tok_n, feat), BF16),
        jax.ShapeDtypeStruct((tok_n, feat), BF16),
        jax.ShapeDtypeStruct((1, feat, hid), BF16),
        jax.ShapeDtypeStruct((1, feat, hid), BF16),
        jax.ShapeDtypeStruct((1, hid, feat), BF16),
    )
    outs = pl.pallas_call(
        functools.partial(kernel, n_exp, n_z),
        out_shape=tuple(pltpu.VMEM(s.shape, s.dtype) for s in shapes),
        in_specs=[hbm, hbm, vm, vm, sm, hbm, hbm, hbm],
        out_specs=[vm] * 5,
        scratch_shapes=[
            pltpu.VMEM((tok_n, feat), BF16),
            pltpu.VMEM((tok_n, feat), BF16),
            pltpu.VMEM((2 * feat, hid), BF16),
            pltpu.VMEM((2 * feat, hid), BF16),
            pltpu.VMEM((2, hid, feat), BF16),
            pltpu.VMEM((CH, n_exp, 2 * SL, feat), BF16),
            pltpu.VMEM((CH, 2, n_src, 2 * SL, feat), BF16),
            pltpu.VMEM((2, CH, 2 * SL, feat), BF16),
            pltpu.VMEM((2, CH * rows, feat), BF16),
            pltpu.VMEM((2, CH * rows, feat), BF16),
            pltpu.VMEM((CH, n_z, 2, 3 * zr, hh), BF16),
            pltpu.VMEM((CH, 2, 2, half, 3 * zr, hh), BF16),
            pltpu.VMEM((CH, n_z, 2, 3 * zr, hh), BF16),
            pltpu.VMEM((CH, 2, n_src, 2 * SL, feat), BF16),
            pltpu.VMEM((CH, n_exp, 2 * SL, feat), BF16),
            pltpu.VMEM((CH, 3, tok_n, n_exp * 2 * SL), BF16),
            pltpu.VMEM((2, tok_n, feat), F32),
            pltpu.VMEM((2, feat, hid), F32),
            pltpu.VMEM((hid, feat), F32),
            pltpu.VMEM((CH, n_z, 2, 3 * zr, hh), BF16),
            pltpu.VMEM((CH * rows, feat), BF16),
            pltpu.VMEM((CH * rows, feat), BF16),
            dma((2,)),
            dma((3,)), dma((3,)), dma((3,)),
            dma((CH,)), dma((CH,)),
            dma((CH,)), dma((CH, 2, 2, half)),
            dma((CH,)), dma((CH, 2, 2, half)),
            dma((CH,)), dma((CH,)),
            dma((CH, 2)), dma((CH, 2)),
            dma((CH,)), dma((CH,)),
        ],
        compiler_params=pltpu.CompilerParams(
            collective_id=0, has_side_effects=True, vmem_limit_bytes=63000 * 1024
        ),
    )(tokens, cotangent, route.T, prob.T, quota, w_gate, w_up, w_down)
    return pl.pallas_call(
        finish,
        out_shape=shapes,
        in_specs=[vm] * 5,
        out_specs=[hbm] * 5,
        scratch_shapes=[dma((5,))],
        compiler_params=pltpu.CompilerParams(vmem_limit_bytes=8 * 1024 * 1024),
    )(*outs)


def solution(mesh):
    placed = (
        P("expert", "dp"),
        P("expert", "dp"),
        P("expert", None),
        P("expert", None),
        P(),
        P("expert", "dp", None),
        P("expert", "dp", None),
        P("expert", None, "dp"),
    )
    return jax.shard_map(
        local,
        mesh=mesh,
        in_specs=placed,
        out_specs=(
            P("expert", "dp"),
            P("expert", "dp"),
            P("expert", "dp", None),
            P("expert", "dp", None),
            P("expert", None, "dp"),
        ),
        check_vma=False,
    )
```

```python
import functools

import jax
import jax.numpy as jnp
from jax import lax
from jax.experimental import pallas as pl
from jax.experimental.pallas import tpu as pltpu
from jax.sharding import PartitionSpec as P

QHI = 24
CH = 3
SL = QHI // CH
MESH = pl.DeviceIdType.MESH
F32 = jnp.float32
BF16 = jnp.bfloat16
ROWS = (((0,), (0,)), ((), ()))
COLS = (((1,), (1,)), ((), ()))


def dot(a, b, dims=(((1,), (0,)), ((), ()))):
    return lax.dot_general(a, b, dims, preferred_element_type=F32)


ARRIVE, BUSY, FLIGHT, LAG = 6.5, 2.0, 2.0, 5


def stage_order(count):
    ready, stage, link, order = [ARRIVE * (c + 1) for c in range(CH)], [0] * CH, 0.0, []
    while len(order) < CH * count:
        c = min((c for c in range(CH) if stage[c] < count), key=lambda c: (ready[c], c))
        order.append((c, stage[c]))
        link = max(link, ready[c]) + BUSY
        ready[c] = link + FLIGHT
        stage[c] += 1
    return order


def kernel(
    n_exp, n_z,
    tok_in, cot_in, route, prob, quota, wg_in, wu_in, wd_in,
    mixed, gtok, ggate, gup, gdown,
    tokens, cot,
    wg, wu, wd, send, recv, trash, xs, gs, part, rsr, ag, outb, cbuf,
    wmat, mixacc, gacc, gdacc, agx, xsx, gsx,
    t_loc, w_loc, w_snd, w_rcv, d_snd, d_rcv, rs_snd, rs_rcv, ag_snd, ag_rcv,
    c_snd, c_rcv, x_snd, x_rcv, m_snd, m_rcv,
):
    dp = lax.axis_index("dp")
    me = lax.axis_index("expert")
    z = dp // 2
    core = lax.rem(dp, 2)
    par = lax.rem(me, 2)
    n_src = n_exp // 2
    half = n_z // 2
    tok_n, feat = tokens.shape
    hid = wg.shape[1]
    hh = hid // 2
    rows = n_src * SL
    zr = rows // n_z
    per = zr // SL
    lanes = 128

    def dev(e, zz, cc):
        return {"expert": e, "dp": zz * 2 + cc}

    right, left = lax.rem(z + 1, n_z), lax.rem(z + n_z - 1, n_z)

    loads = [
        pltpu.make_async_copy(tok_in, tokens, t_loc.at[0]),
        pltpu.make_async_copy(cot_in, cot, t_loc.at[1]),
    ]
    for copy in loads:
        copy.start()

    barrier = pltpu.get_barrier_semaphore()

    def greet(e, zz, cc):
        pl.semaphore_signal(barrier, inc=1, device_id=dev(e, zz, cc), device_id_type=MESH)

    greet(me, right, core)
    greet(me, left, core)

    @pl.loop(1, n_exp)
    def _(t):
        greet(lax.rem(me + t, n_exp), z, par)

    @pl.when(core != par)
    def _():
        greet(me, z, par)

    @pl.loop(0, n_src)
    def _(t):
        greet(2 * t + core, z, 1 - par)

    own = [
        pltpu.make_async_copy(wg_in.at[0], wg.at[pl.ds(core * feat, feat)], w_loc.at[0]),
        pltpu.make_async_copy(wu_in.at[0], wu.at[pl.ds(core * feat, feat)], w_loc.at[1]),
        pltpu.make_async_copy(wd_in.at[0], wd.at[core], w_loc.at[2]),
    ]
    for copy in own:
        copy.start()

    mine = lax.broadcasted_iota(jnp.int32, (n_exp, tok_n), 0)
    match = jnp.zeros((n_exp, tok_n), F32)
    pe_t = jnp.zeros((n_exp, tok_n), F32)
    for k in range(route.shape[0]):
        hit = route[k : k + 1] == mine
        match = jnp.where(hit, 1.0, match)
        pe_t = jnp.where(hit, prob[k : k + 1], pe_t)
    earlier = lax.broadcasted_iota(jnp.int32, (tok_n, tok_n), 0) < lax.broadcasted_iota(
        jnp.int32, (tok_n, tok_n), 1
    )
    before = dot(match.astype(BF16), earlier.astype(F32).astype(BF16))
    row1 = lax.broadcasted_iota(jnp.int32, (n_exp, 1), 0)
    quotas = jnp.zeros((n_exp, 1), jnp.int32)
    for e in range(n_exp):
        quotas = jnp.where(row1 == e, quota[e], quotas)
    eff_t = jnp.where((match > 0.0) & (before < quotas.astype(F32)), before, 255.0)
    for copy in loads:
        copy.wait()

    shared = [
        (wg_in.at[0], wg.at[pl.ds(core * feat, feat)]),
        (wu_in.at[0], wu.at[pl.ds(core * feat, feat)]),
        (wd_in.at[0], wd.at[core]),
    ]

    def weight_copy(i):
        return pltpu.make_async_remote_copy(
            src_ref=shared[i][0], dst_ref=shared[i][1], send_sem=w_snd.at[i], recv_sem=w_rcv.at[i],
            device_id=dev(me, z, 1 - core), device_id_type=MESH,
        )

    slot = lax.broadcasted_iota(jnp.int32, (n_exp, SL, tok_n), 1).astype(F32)

    def fill(c):
        hit = eff_t[:, None, :] == slot + float(c * SL)
        pick = jnp.where(hit, 1.0, 0.0).reshape(n_exp * SL, tok_n)
        weight = jnp.where(hit, pe_t[:, None, :], 0.0).reshape(n_exp * SL, tok_n)
        slot_prob = jnp.sum(weight, axis=1, keepdims=True)
        pick = pick.astype(BF16)
        picked = dot(pick, tokens[...]).reshape(n_exp, SL, feat)
        grads = (dot(pick, cot[...]) * slot_prob).reshape(n_exp, SL, feat)
        send[c] = jnp.concatenate([picked, grads], axis=1).astype(BF16)

    def dispatch(c):
        def to_expert(e):
            return pltpu.make_async_remote_copy(
                src_ref=send.at[c, e], dst_ref=recv.at[c, core, me // 2],
                send_sem=d_snd.at[c], recv_sem=d_rcv.at[c],
                device_id=dev(e, z, par), device_id_type=MESH,
            )

        @pl.loop(1, n_exp // 2)
        def _(t):
            to_expert(lax.rem(me + t, n_exp)).start()
            to_expert(lax.rem(me + n_exp - t, n_exp)).start()

        to_expert(lax.rem(me + n_exp // 2, n_exp)).start()

        @pl.when(core != par)
        def _():
            to_expert(me).start()

        @pl.when(core == par)
        def _():
            pltpu.make_async_copy(send.at[c, me], recv.at[c, core, me // 2], d_rcv.at[c]).start()
            pltpu.make_async_copy(send.at[c, me], trash.at[0, c], d_snd.at[c]).start()

    fill(0)
    others = par == core
    pl.semaphore_wait(barrier, n_exp + n_src + 2 - others.astype(jnp.int32))
    dispatch(0)
    for i in range(3):
        weight_copy(i).start()
    for c in range(1, CH):
        fill(c)
        dispatch(c)
    for copy in own:
        copy.wait()
    for i in range(3):
        weight_copy(i).wait_recv()

    wide = n_exp * 2 * SL

    def tables(c):
        fill = jnp.zeros((lanes - n_exp, tok_n), F32)
        eff = jnp.concatenate([eff_t, fill], axis=0).T.astype(BF16)
        pe = jnp.concatenate([pe_t, fill], axis=0).T
        spread = (
            lax.broadcasted_iota(jnp.int32, (lanes, wide), 1) // (2 * SL)
            == lax.broadcasted_iota(jnp.int32, (lanes, wide), 0)
        ).astype(F32).astype(BF16)
        pe_hi = pe.astype(BF16)
        pe_lo = (pe - pe_hi.astype(F32)).astype(BF16)
        eff_x = dot(eff, spread)
        place = lax.rem(lax.broadcasted_iota(jnp.int32, (tok_n, wide), 1), 2 * SL)
        hit = eff_x == (lax.rem(place, SL) + c * SL).astype(F32)
        out_hit = hit & (place < SL)
        wmat[c, 0] = jnp.where(out_hit, dot(pe_hi, spread), 0.0).astype(BF16)
        wmat[c, 1] = jnp.where(out_hit, dot(pe_lo, spread), 0.0).astype(BF16)
        wmat[c, 2] = jnp.where(hit & (place >= SL), 1.0, 0.0).astype(BF16)

    def away(way, k):
        return lax.rem(z + k, n_z) if way == 0 else lax.rem(z + n_z - k, n_z)

    def longest(h, way):
        return half if way == h else half - 1

    def rs_copy(c, h, way, k):
        return pltpu.make_async_remote_copy(
            src_ref=part.at[c, away(way, k), h], dst_ref=rsr.at[c, h, way, k - 1],
            send_sem=rs_snd.at[c], recv_sem=rs_rcv.at[c, h, way, k - 1],
            device_id=dev(me, (right, left)[way], core), device_id_type=MESH,
        )

    def rs_landed(c, h, way, k):
        ref = rsr.at[c, h, way, k - 1]
        return pltpu.make_async_copy(ref, ref, rs_rcv.at[c, h, way, k - 1])

    def ag_copy(c, h, way, k):
        ref = ag.at[c, away(1 - way, k), h]
        return pltpu.make_async_remote_copy(
            src_ref=ref, dst_ref=ref, send_sem=ag_snd.at[c], recv_sem=ag_rcv.at[c, h, way, k],
            device_id=dev(me, (right, left)[way], core), device_id_type=MESH,
        )

    def ag_landed(c, h, way, k):
        ref = ag.at[c, away(1 - way, k + 1), h]
        return pltpu.make_async_copy(ref, ref, ag_rcv.at[c, h, way, k])

    def first(c):
        pltpu.make_async_copy(recv.at[c], recv.at[c], d_rcv.at[c]).wait()
        gate = up = back = None
        for b in range(2):
            both = recv[c, b].astype(F32)
            x = both[:, :SL].reshape(rows, feat).astype(BF16)
            g = both[:, SL:].reshape(rows, feat).astype(BF16)
            xs[b, c * rows : (c + 1) * rows] = x
            gs[b, c * rows : (c + 1) * rows] = g
        x = jnp.concatenate([xs[0, c * rows : (c + 1) * rows], xs[1, c * rows : (c + 1) * rows]], axis=1)
        for h in range(2):
            cols = slice(h * hh, (h + 1) * hh)
            gate = dot(x, wg[:, cols]).astype(BF16).reshape(n_z, zr, hh)
            up = dot(x, wu[:, cols]).astype(BF16).reshape(n_z, zr, hh)
            back = dot(gs[0, c * rows : (c + 1) * rows], wd[0, cols], COLS)
            back = back + dot(gs[1, c * rows : (c + 1) * rows], wd[1, cols], COLS)
            back = back.astype(BF16).reshape(n_z, zr, hh)
            part[c, :, h, 0:zr] = gate
            part[c, :, h, zr : 2 * zr] = up
            part[c, :, h, 2 * zr : 3 * zr] = back
            for way in (h, 1 - h):
                rs_copy(c, h, way, longest(h, way)).start()
        for i in range(2):
            x_copy(c, i).start()

    def to_sibling(src, dst, snd, rcv):
        return pltpu.make_async_remote_copy(
            src_ref=src, dst_ref=dst, send_sem=snd, recv_sem=rcv,
            device_id=dev(me, z, 1 - core), device_id_type=MESH,
        )

    def x_copy(c, i):
        src, dst = ((xs, xsx), (gs, gsx))[i]
        part_rows = pl.ds(c * rows, rows)
        return to_sibling(src.at[1 - core, part_rows], dst.at[part_rows], x_snd.at[c, i], x_rcv.at[c, i])

    def block_at(p):
        return away(p % 2, (p + 1) // 2)

    def m_copy(c, p):
        d = block_at(p)
        return to_sibling(ag.at[c, d], agx.at[c, d], m_snd.at[c], m_rcv.at[c])

    def rs_hop(c, step):
        for h in range(2):
            for way in (h, 1 - h):
                k = longest(h, way) - step
                if k >= 1:
                    rs_landed(c, h, way, k + 1).wait()
                    d = away(way, k)
                    part[c, d, h] = (part[c, d, h].astype(F32) + rsr[c, h, way, k].astype(F32)).astype(BF16)
                    rs_copy(c, h, way, k).start()

    def middle(c):
        for h in range(2):
            for way in (1 - h, h):
                rs_landed(c, h, way, 1).wait()
            total = part[c, z, h].astype(F32) + rsr[c, h, 0, 0].astype(F32) + rsr[c, h, 1, 0].astype(F32)
            gate, up, back = total[0:zr], total[zr : 2 * zr], total[2 * zr :]
            sig = jax.nn.sigmoid(gate)
            act = gate * sig
            ag[c, z, h, 0:zr] = (act * up).astype(BF16)
            ag[c, z, h, zr : 2 * zr] = (back * up * sig * (1.0 + gate * (1.0 - sig))).astype(BF16)
            ag[c, z, h, 2 * zr : 3 * zr] = (back * act).astype(BF16)
            for way in (h, 1 - h):
                ag_copy(c, h, way, 0).start()
        stream(c, [0])

    def ag_hop(c, step):
        for h in range(2):
            for way in (h, 1 - h):
                if step < longest(h, way):
                    ag_landed(c, h, way, step - 1).wait()
                    ag_copy(c, h, way, step).start()
                else:
                    ag_landed(c, h, way, step - 1).wait()
        stream(c, [2 * step - 1, 2 * step])

    def piece(c, i, h, held=ag):
        return held[c, :, h, i * zr : (i + 1) * zr].reshape(rows, hh)

    def to_token(c, i, b):
        return pltpu.make_async_remote_copy(
            src_ref=outb.at[c, b, i], dst_ref=cbuf.at[c, me],
            send_sem=c_snd.at[c], recv_sem=c_rcv.at[c],
            device_id=dev(2 * i + core, z, b), device_id_type=MESH,
        )

    def to_self(c):
        pltpu.make_async_copy(outb.at[c, core, me // 2], cbuf.at[c, me], c_rcv.at[c]).start()
        pltpu.make_async_copy(outb.at[c, core, me // 2], trash.at[1, c], c_snd.at[c]).start()

    def products(get, b):
        out = back = None
        for h in range(2):
            cols = slice(h * hh, (h + 1) * hh)
            fs = slice(b * feat, (b + 1) * feat)
            o = dot(get(0, h), wd[b, cols])
            r = dot(get(1, h), wg[fs, cols], COLS) + dot(get(2, h), wu[fs, cols], COLS)
            out = o if out is None else out + o
            back = r if back is None else back + r
        both = [v.reshape(v.shape[0] // SL, SL, feat) for v in (out, back)]
        return jnp.concatenate(both, axis=1).astype(BF16)

    def stream(c, places):
        ds = [block_at(p) for p in places]
        for p in places:
            m_copy(c, p).start()

        def get(i, h):
            return jnp.concatenate([ag[c, d, h, i * zr : (i + 1) * zr] for d in ds], axis=0)

        for b in range(2):
            both = products(get, b)
            for q, d in enumerate(ds):
                for r in range(per):
                    outb[c, b, d * per + r] = both[q * per + r]
        for d in ds:
            for r in range(per):
                i = d * per + r
                mine_too = (par == core) & (i == me // 2)
                for b in range(2):
                    here = mine_too & (core == b)

                    @pl.when(jnp.logical_not(here))
                    def _():
                        to_token(c, i, b).start()

                    @pl.when(here)
                    def _():
                        to_self(c)

    def last(c):
        for h in range(2):
            ag_landed(c, h, h, half - 1).wait()
        stream(c, [n_z - 1])

    def weight_grads(c):
        for i in range(2):
            x_copy(c, i).wait_recv()
        pltpu.make_async_copy(agx.at[c], agx.at[c], m_rcv.at[c]).wait()
        part_rows = slice(c * rows, (c + 1) * rows)
        x = jnp.concatenate([xs[core, part_rows], xsx[part_rows]], axis=0)
        g = jnp.concatenate([gs[core, part_rows], gsx[part_rows]], axis=0)
        for h in range(2):
            cols = slice(h * hh, (h + 1) * hh)
            hidden, pre, up = (
                jnp.concatenate([piece(c, i, h), piece(c, i, h, agx)], axis=0) for i in range(3)
            )
            sums = [dot(x, pre, ROWS), dot(x, up, ROWS), dot(hidden, g, ROWS)]
            refs = [gacc.at[0, :, cols], gacc.at[1, :, cols], gdacc.at[cols]]
            outs = [ggate.at[0, :, cols], gup.at[0, :, cols], gdown.at[0, cols]]
            for total, ref, out in zip(sums, refs, outs):
                if c > 0:
                    total = total + ref[...]
                if c < CH - 1:
                    ref[...] = total
                else:
                    out[...] = total.astype(BF16)

    def sent(c):
        for ref, sem in (
            (send.at[c], d_snd), (outb.at[c], c_snd), (ag.at[c], m_snd),
            (part.at[c, 0 : n_z - 1], rs_snd), (ag.at[c, 0 : n_z - 1], ag_snd),
        ):
            pltpu.make_async_copy(ref, ref, sem.at[c]).wait()
        for i in range(2):
            x_copy(c, i).wait_send()

    def mix(c):
        pltpu.make_async_copy(cbuf.at[c], cbuf.at[c], c_rcv.at[c]).wait()
        got = cbuf[c].reshape(wide, feat)
        m = dot(wmat[c, 0], got) + dot(wmat[c, 1], got)
        g = dot(wmat[c, 2], got)
        if c > 0:
            m, g = m + mixacc[0], g + mixacc[1]
        if c < CH - 1:
            mixacc[0], mixacc[1] = m, g
        else:
            mixed[...], gtok[...] = m.astype(BF16), g.astype(BF16)

    stages = [first]
    for s in range(1, half):
        stages.append(functools.partial(rs_hop, step=s))
    stages.append(middle)
    for s in range(1, half):
        stages.append(functools.partial(ag_hop, step=s))
    stages.append(last)
    order = stage_order(len(stages))
    place = {(c, stage): n for n, (c, stage) in enumerate(order)}
    after = [[] for _ in order]
    for c in range(CH):
        over = place[(c, len(stages) - 1)]
        after[min(over + 1, len(order) - 1)].append(functools.partial(weight_grads, c))
        after[min(over + LAG, len(order) - 1)].append(functools.partial(mix, c))
        after[place[(0, 2 + c)]].append(functools.partial(tables, c))
    for n, (c, stage) in enumerate(order):
        stages[stage](c)
        for task in after[n]:
            task()

    for c in range(CH):
        sent(c)
    for i in range(3):
        weight_copy(i).wait_send()


def finish(*refs):
    ins, outs, sem = refs[:5], refs[5:10], refs[10]
    copies = [pltpu.make_async_copy(src, dst, sem.at[i]) for i, (src, dst) in enumerate(zip(ins, outs))]
    for copy in copies:
        copy.start()
    for copy in copies:
        copy.wait()


def local(tokens, cotangent, route, prob, quota, w_gate, w_up, w_down):
    n_exp = lax.axis_size("expert")
    n_z = lax.axis_size("dp") // 2
    tok_n, feat = tokens.shape
    hid = w_gate.shape[2]
    half = n_z // 2
    n_src = n_exp // 2
    rows = n_src * SL
    zr = rows // n_z
    hh = hid // 2
    vm = pl.BlockSpec(memory_space=pltpu.VMEM)
    hbm = pl.BlockSpec(memory_space=pltpu.HBM)
    sm = pl.BlockSpec(memory_space=pltpu.SMEM)
    dma = pltpu.SemaphoreType.DMA
    shapes = (
        jax.ShapeDtypeStruct((tok_n, feat), BF16),
        jax.ShapeDtypeStruct((tok_n, feat), BF16),
        jax.ShapeDtypeStruct((1, feat, hid), BF16),
        jax.ShapeDtypeStruct((1, feat, hid), BF16),
        jax.ShapeDtypeStruct((1, hid, feat), BF16),
    )
    outs = pl.pallas_call(
        functools.partial(kernel, n_exp, n_z),
        out_shape=tuple(pltpu.VMEM(s.shape, s.dtype) for s in shapes),
        in_specs=[hbm, hbm, vm, vm, sm, hbm, hbm, hbm],
        out_specs=[vm] * 5,
        scratch_shapes=[
            pltpu.VMEM((tok_n, feat), BF16),
            pltpu.VMEM((tok_n, feat), BF16),
            pltpu.VMEM((2 * feat, hid), BF16),
            pltpu.VMEM((2 * feat, hid), BF16),
            pltpu.VMEM((2, hid, feat), BF16),
            pltpu.VMEM((CH, n_exp, 2 * SL, feat), BF16),
            pltpu.VMEM((CH, 2, n_src, 2 * SL, feat), BF16),
            pltpu.VMEM((2, CH, 2 * SL, feat), BF16),
            pltpu.VMEM((2, CH * rows, feat), BF16),
            pltpu.VMEM((2, CH * rows, feat), BF16),
            pltpu.VMEM((CH, n_z, 2, 3 * zr, hh), BF16),
            pltpu.VMEM((CH, 2, 2, half, 3 * zr, hh), BF16),
            pltpu.VMEM((CH, n_z, 2, 3 * zr, hh), BF16),
            pltpu.VMEM((CH, 2, n_src, 2 * SL, feat), BF16),
            pltpu.VMEM((CH, n_exp, 2 * SL, feat), BF16),
            pltpu.VMEM((CH, 3, tok_n, n_exp * 2 * SL), BF16),
            pltpu.VMEM((2, tok_n, feat), F32),
            pltpu.VMEM((2, feat, hid), F32),
            pltpu.VMEM((hid, feat), F32),
            pltpu.VMEM((CH, n_z, 2, 3 * zr, hh), BF16),
            pltpu.VMEM((CH * rows, feat), BF16),
            pltpu.VMEM((CH * rows, feat), BF16),
            dma((2,)),
            dma((3,)), dma((3,)), dma((3,)),
            dma((CH,)), dma((CH,)),
            dma((CH,)), dma((CH, 2, 2, half)),
            dma((CH,)), dma((CH, 2, 2, half)),
            dma((CH,)), dma((CH,)),
            dma((CH, 2)), dma((CH, 2)),
            dma((CH,)), dma((CH,)),
        ],
        compiler_params=pltpu.CompilerParams(
            collective_id=0, has_side_effects=True, vmem_limit_bytes=63000 * 1024
        ),
    )(tokens, cotangent, route.T, prob.T, quota, w_gate, w_up, w_down)
    return pl.pallas_call(
        finish,
        out_shape=shapes,
        in_specs=[vm] * 5,
        out_specs=[hbm] * 5,
        scratch_shapes=[dma((5,))],
        compiler_params=pltpu.CompilerParams(vmem_limit_bytes=8 * 1024 * 1024),
    )(*outs)


def solution(mesh):
    placed = (
        P("expert", "dp"),
        P("expert", "dp"),
        P("expert", None),
        P("expert", None),
        P(),
        P("expert", "dp", None),
        P("expert", "dp", None),
        P("expert", None, "dp"),
    )
    return jax.shard_map(
        local,
        mesh=mesh,
        in_specs=placed,
        out_specs=(
            P("expert", "dp"),
            P("expert", "dp"),
            P("expert", "dp", None),
            P("expert", "dp", None),
            P("expert", None, "dp"),
        ),
        check_vma=False,
    )
```

```python
import functools

import jax
import jax.numpy as jnp
from jax import lax
from jax.experimental import pallas as pl
from jax.experimental.pallas import tpu as pltpu
from jax.sharding import PartitionSpec as P

QHI = 24
CH = 3
SL = QHI // CH
MESH = pl.DeviceIdType.MESH
F32 = jnp.float32
BF16 = jnp.bfloat16
ROWS = (((0,), (0,)), ((), ()))
COLS = (((1,), (1,)), ((), ()))


def dot(a, b, dims=(((1,), (0,)), ((), ()))):
    return lax.dot_general(a, b, dims, preferred_element_type=F32)


ARRIVE, BUSY, FLIGHT, LAG = 6.5, 2.0, 2.0, 5


def stage_order(count):
    ready, stage, link, order = [ARRIVE * (c + 1) for c in range(CH)], [0] * CH, 0.0, []
    while len(order) < CH * count:
        c = min((c for c in range(CH) if stage[c] < count), key=lambda c: (ready[c], c))
        order.append((c, stage[c]))
        link = max(link, ready[c]) + BUSY
        ready[c] = link + FLIGHT
        stage[c] += 1
    return order


def kernel(
    n_exp, n_z,
    tok_in, cot_in, route, prob, quota, wg_in, wu_in, wd_in,
    mixed, gtok, ggate, gup, gdown,
    tokens, cot,
    wg, wu, wd, send, recv, trash, xs, gs, part, rsr, ag, outb, cbuf,
    wmat, mixacc, gacc, gdacc, agx, xsx, gsx,
    t_loc, w_loc, w_snd, w_rcv, d_snd, d_rcv, rs_snd, rs_rcv, ag_snd, ag_rcv,
    c_snd, c_rcv, x_snd, x_rcv, m_snd, m_rcv,
):
    dp = lax.axis_index("dp")
    me = lax.axis_index("expert")
    z = dp // 2
    core = lax.rem(dp, 2)
    par = lax.rem(me, 2)
    n_src = n_exp // 2
    half = n_z // 2
    tok_n, feat = tokens.shape
    hid = wg.shape[1]
    hh = hid // 2
    rows = n_src * SL
    zr = rows // n_z
    per = zr // SL
    lanes = 128

    def dev(e, zz, cc):
        return {"expert": e, "dp": zz * 2 + cc}

    right, left = lax.rem(z + 1, n_z), lax.rem(z + n_z - 1, n_z)

    loads = [
        pltpu.make_async_copy(tok_in, tokens, t_loc.at[0]),
        pltpu.make_async_copy(cot_in, cot, t_loc.at[1]),
    ]
    for copy in loads:
        copy.start()

    barrier = pltpu.get_barrier_semaphore()

    def greet(e, zz, cc):
        pl.semaphore_signal(barrier, inc=1, device_id=dev(e, zz, cc), device_id_type=MESH)

    greet(me, right, core)
    greet(me, left, core)

    @pl.loop(1, n_exp)
    def _(t):
        greet(lax.rem(me + t, n_exp), z, par)

    @pl.when(core != par)
    def _():
        greet(me, z, par)

    @pl.loop(0, n_src)
    def _(t):
        greet(2 * t + core, z, 1 - par)

    own = [
        pltpu.make_async_copy(wg_in.at[0], wg.at[pl.ds(core * feat, feat)], w_loc.at[0]),
        pltpu.make_async_copy(wu_in.at[0], wu.at[pl.ds(core * feat, feat)], w_loc.at[1]),
        pltpu.make_async_copy(wd_in.at[0], wd.at[core], w_loc.at[2]),
    ]
    for copy in own:
        copy.start()

    mine = lax.broadcasted_iota(jnp.int32, (n_exp, tok_n), 0)
    match = jnp.zeros((n_exp, tok_n), F32)
    pe_t = jnp.zeros((n_exp, tok_n), F32)
    for k in range(route.shape[0]):
        hit = route[k : k + 1] == mine
        match = jnp.where(hit, 1.0, match)
        pe_t = jnp.where(hit, prob[k : k + 1], pe_t)
    earlier = lax.broadcasted_iota(jnp.int32, (tok_n, tok_n), 0) < lax.broadcasted_iota(
        jnp.int32, (tok_n, tok_n), 1
    )
    before = dot(match.astype(BF16), earlier.astype(F32).astype(BF16))
    row1 = lax.broadcasted_iota(jnp.int32, (n_exp, 1), 0)
    quotas = jnp.zeros((n_exp, 1), jnp.int32)
    for e in range(n_exp):
        quotas = jnp.where(row1 == e, quota[e], quotas)
    eff_t = jnp.where((match > 0.0) & (before < quotas.astype(F32)), before, 255.0)
    for copy in loads:
        copy.wait()

    shared = [
        (wg_in.at[0], wg.at[pl.ds(core * feat, feat)]),
        (wu_in.at[0], wu.at[pl.ds(core * feat, feat)]),
        (wd_in.at[0], wd.at[core]),
    ]

    def weight_copy(i):
        return pltpu.make_async_remote_copy(
            src_ref=shared[i][0], dst_ref=shared[i][1], send_sem=w_snd.at[i], recv_sem=w_rcv.at[i],
            device_id=dev(me, z, 1 - core), device_id_type=MESH,
        )

    slot = lax.broadcasted_iota(jnp.int32, (n_exp, SL, tok_n), 1).astype(F32)

    def fill(c):
        hit = eff_t[:, None, :] == slot + float(c * SL)
        pick = jnp.where(hit, 1.0, 0.0).reshape(n_exp * SL, tok_n)
        weight = jnp.where(hit, pe_t[:, None, :], 0.0).reshape(n_exp * SL, tok_n)
        slot_prob = jnp.sum(weight, axis=1, keepdims=True)
        pick = pick.astype(BF16)
        picked = dot(pick, tokens[...]).reshape(n_exp, SL, feat)
        grads = (dot(pick, cot[...]) * slot_prob).reshape(n_exp, SL, feat)
        send[c] = jnp.concatenate([picked, grads], axis=1).astype(BF16)

    def dispatch(c):
        def to_expert(e):
            return pltpu.make_async_remote_copy(
                src_ref=send.at[c, e], dst_ref=recv.at[c, core, me // 2],
                send_sem=d_snd.at[c], recv_sem=d_rcv.at[c],
                device_id=dev(e, z, par), device_id_type=MESH,
            )

        @pl.loop(1, n_exp // 2, unroll=True)
        def _(t):
            to_expert(lax.rem(me + t, n_exp)).start()
            to_expert(lax.rem(me + n_exp - t, n_exp)).start()

        to_expert(lax.rem(me + n_exp // 2, n_exp)).start()

        @pl.when(core != par)
        def _():
            to_expert(me).start()

        @pl.when(core == par)
        def _():
            pltpu.make_async_copy(send.at[c, me], recv.at[c, core, me // 2], d_rcv.at[c]).start()
            pltpu.make_async_copy(send.at[c, me], trash.at[0, c], d_snd.at[c]).start()

    fill(0)
    others = par == core
    pl.semaphore_wait(barrier, n_exp + n_src + 2 - others.astype(jnp.int32))
    dispatch(0)
    for i in range(3):
        weight_copy(i).start()
    for c in range(1, CH):
        fill(c)
        dispatch(c)
    for copy in own:
        copy.wait()
    for i in range(3):
        weight_copy(i).wait_recv()

    wide = n_exp * 2 * SL

    def tables(c):
        fill = jnp.zeros((lanes - n_exp, tok_n), F32)
        eff = jnp.concatenate([eff_t, fill], axis=0).T.astype(BF16)
        pe = jnp.concatenate([pe_t, fill], axis=0).T
        spread = (
            lax.broadcasted_iota(jnp.int32, (lanes, wide), 1) // (2 * SL)
            == lax.broadcasted_iota(jnp.int32, (lanes, wide), 0)
        ).astype(F32).astype(BF16)
        pe_hi = pe.astype(BF16)
        pe_lo = (pe - pe_hi.astype(F32)).astype(BF16)
        eff_x = dot(eff, spread)
        place = lax.rem(lax.broadcasted_iota(jnp.int32, (tok_n, wide), 1), 2 * SL)
        hit = eff_x == (lax.rem(place, SL) + c * SL).astype(F32)
        out_hit = hit & (place < SL)
        wmat[c, 0] = jnp.where(out_hit, dot(pe_hi, spread), 0.0).astype(BF16)
        wmat[c, 1] = jnp.where(out_hit, dot(pe_lo, spread), 0.0).astype(BF16)
        wmat[c, 2] = jnp.where(hit & (place >= SL), 1.0, 0.0).astype(BF16)

    def away(way, k):
        return lax.rem(z + k, n_z) if way == 0 else lax.rem(z + n_z - k, n_z)

    def longest(h, way):
        return half if way == h else half - 1

    def rs_copy(c, h, way, k):
        return pltpu.make_async_remote_copy(
            src_ref=part.at[c, away(way, k), h], dst_ref=rsr.at[c, h, way, k - 1],
            send_sem=rs_snd.at[c], recv_sem=rs_rcv.at[c, h, way, k - 1],
            device_id=dev(me, (right, left)[way], core), device_id_type=MESH,
        )

    def rs_landed(c, h, way, k):
        ref = rsr.at[c, h, way, k - 1]
        return pltpu.make_async_copy(ref, ref, rs_rcv.at[c, h, way, k - 1])

    def ag_copy(c, h, way, k):
        ref = ag.at[c, away(1 - way, k), h]
        return pltpu.make_async_remote_copy(
            src_ref=ref, dst_ref=ref, send_sem=ag_snd.at[c], recv_sem=ag_rcv.at[c, h, way, k],
            device_id=dev(me, (right, left)[way], core), device_id_type=MESH,
        )

    def ag_landed(c, h, way, k):
        ref = ag.at[c, away(1 - way, k + 1), h]
        return pltpu.make_async_copy(ref, ref, ag_rcv.at[c, h, way, k])

    def first(c):
        pltpu.make_async_copy(recv.at[c], recv.at[c], d_rcv.at[c]).wait()
        gate = up = back = None
        for b in range(2):
            both = recv[c, b].astype(F32)
            x = both[:, :SL].reshape(rows, feat).astype(BF16)
            g = both[:, SL:].reshape(rows, feat).astype(BF16)
            xs[b, c * rows : (c + 1) * rows] = x
            gs[b, c * rows : (c + 1) * rows] = g
        x = jnp.concatenate([xs[0, c * rows : (c + 1) * rows], xs[1, c * rows : (c + 1) * rows]], axis=1)
        for h in range(2):
            cols = slice(h * hh, (h + 1) * hh)
            gate = dot(x, wg[:, cols]).astype(BF16).reshape(n_z, zr, hh)
            up = dot(x, wu[:, cols]).astype(BF16).reshape(n_z, zr, hh)
            back = dot(gs[0, c * rows : (c + 1) * rows], wd[0, cols], COLS)
            back = back + dot(gs[1, c * rows : (c + 1) * rows], wd[1, cols], COLS)
            back = back.astype(BF16).reshape(n_z, zr, hh)
            part[c, :, h, 0:zr] = gate
            part[c, :, h, zr : 2 * zr] = up
            part[c, :, h, 2 * zr : 3 * zr] = back
            for way in (h, 1 - h):
                rs_copy(c, h, way, longest(h, way)).start()
        for i in range(2):
            x_copy(c, i).start()

    def to_sibling(src, dst, snd, rcv):
        return pltpu.make_async_remote_copy(
            src_ref=src, dst_ref=dst, send_sem=snd, recv_sem=rcv,
            device_id=dev(me, z, 1 - core), device_id_type=MESH,
        )

    def x_copy(c, i):
        src, dst = ((xs, xsx), (gs, gsx))[i]
        part_rows = pl.ds(c * rows, rows)
        return to_sibling(src.at[1 - core, part_rows], dst.at[part_rows], x_snd.at[c, i], x_rcv.at[c, i])

    def block_at(p):
        return away(p % 2, (p + 1) // 2)

    def m_copy(c, p):
        d = block_at(p)
        return to_sibling(ag.at[c, d], agx.at[c, d], m_snd.at[c], m_rcv.at[c])

    def rs_hop(c, step):
        for h in range(2):
            for way in (h, 1 - h):
                k = longest(h, way) - step
                if k >= 1:
                    rs_landed(c, h, way, k + 1).wait()
                    d = away(way, k)
                    part[c, d, h] = (part[c, d, h].astype(F32) + rsr[c, h, way, k].astype(F32)).astype(BF16)
                    rs_copy(c, h, way, k).start()

    def middle(c):
        for h in range(2):
            for way in (1 - h, h):
                rs_landed(c, h, way, 1).wait()
            total = part[c, z, h].astype(F32) + rsr[c, h, 0, 0].astype(F32) + rsr[c, h, 1, 0].astype(F32)
            gate, up, back = total[0:zr], total[zr : 2 * zr], total[2 * zr :]
            sig = jax.nn.sigmoid(gate)
            act = gate * sig
            ag[c, z, h, 0:zr] = (act * up).astype(BF16)
            ag[c, z, h, zr : 2 * zr] = (back * up * sig * (1.0 + gate * (1.0 - sig))).astype(BF16)
            ag[c, z, h, 2 * zr : 3 * zr] = (back * act).astype(BF16)
            for way in (h, 1 - h):
                ag_copy(c, h, way, 0).start()
        stream(c, [0])

    def ag_hop(c, step):
        for h in range(2):
            for way in (h, 1 - h):
                if step < longest(h, way):
                    ag_landed(c, h, way, step - 1).wait()
                    ag_copy(c, h, way, step).start()
                else:
                    ag_landed(c, h, way, step - 1).wait()
        stream(c, [2 * step - 1, 2 * step])

    def piece(c, i, h, held=ag):
        return held[c, :, h, i * zr : (i + 1) * zr].reshape(rows, hh)

    def to_token(c, i, b):
        return pltpu.make_async_remote_copy(
            src_ref=outb.at[c, b, i], dst_ref=cbuf.at[c, me],
            send_sem=c_snd.at[c], recv_sem=c_rcv.at[c],
            device_id=dev(2 * i + core, z, b), device_id_type=MESH,
        )

    def to_self(c):
        pltpu.make_async_copy(outb.at[c, core, me // 2], cbuf.at[c, me], c_rcv.at[c]).start()
        pltpu.make_async_copy(outb.at[c, core, me // 2], trash.at[1, c], c_snd.at[c]).start()

    def products(get, b):
        out = back = None
        for h in range(2):
            cols = slice(h * hh, (h + 1) * hh)
            fs = slice(b * feat, (b + 1) * feat)
            o = dot(get(0, h), wd[b, cols])
            r = dot(get(1, h), wg[fs, cols], COLS) + dot(get(2, h), wu[fs, cols], COLS)
            out = o if out is None else out + o
            back = r if back is None else back + r
        both = [v.reshape(v.shape[0] // SL, SL, feat) for v in (out, back)]
        return jnp.concatenate(both, axis=1).astype(BF16)

    def stream(c, places):
        ds = [block_at(p) for p in places]
        for p in places:
            m_copy(c, p).start()

        def get(i, h):
            return jnp.concatenate([ag[c, d, h, i * zr : (i + 1) * zr] for d in ds], axis=0)

        for b in range(2):
            both = products(get, b)
            for q, d in enumerate(ds):
                for r in range(per):
                    outb[c, b, d * per + r] = both[q * per + r]
        for d in ds:
            for r in range(per):
                i = d * per + r
                mine_too = (par == core) & (i == me // 2)
                for b in range(2):
                    here = mine_too & (core == b)

                    @pl.when(jnp.logical_not(here))
                    def _():
                        to_token(c, i, b).start()

                    @pl.when(here)
                    def _():
                        to_self(c)

    def last(c):
        for h in range(2):
            ag_landed(c, h, h, half - 1).wait()
        stream(c, [n_z - 1])

    def weight_grads(c):
        for i in range(2):
            x_copy(c, i).wait_recv()
        pltpu.make_async_copy(agx.at[c], agx.at[c], m_rcv.at[c]).wait()
        part_rows = slice(c * rows, (c + 1) * rows)
        x = jnp.concatenate([xs[core, part_rows], xsx[part_rows]], axis=0)
        g = jnp.concatenate([gs[core, part_rows], gsx[part_rows]], axis=0)
        for h in range(2):
            cols = slice(h * hh, (h + 1) * hh)
            hidden, pre, up = (
                jnp.concatenate([piece(c, i, h), piece(c, i, h, agx)], axis=0) for i in range(3)
            )
            sums = [dot(x, pre, ROWS), dot(x, up, ROWS), dot(hidden, g, ROWS)]
            refs = [gacc.at[0, :, cols], gacc.at[1, :, cols], gdacc.at[cols]]
            outs = [ggate.at[0, :, cols], gup.at[0, :, cols], gdown.at[0, cols]]
            for total, ref, out in zip(sums, refs, outs):
                if c > 0:
                    total = total + ref[...]
                if c < CH - 1:
                    ref[...] = total
                else:
                    out[...] = total.astype(BF16)

    def sent(c):
        for ref, sem in (
            (send.at[c], d_snd), (outb.at[c], c_snd), (ag.at[c], m_snd),
            (part.at[c, 0 : n_z - 1], rs_snd), (ag.at[c, 0 : n_z - 1], ag_snd),
        ):
            pltpu.make_async_copy(ref, ref, sem.at[c]).wait()
        for i in range(2):
            x_copy(c, i).wait_send()

    def mix(c):
        pltpu.make_async_copy(cbuf.at[c], cbuf.at[c], c_rcv.at[c]).wait()
        got = cbuf[c].reshape(wide, feat)
        m = dot(wmat[c, 0], got) + dot(wmat[c, 1], got)
        g = dot(wmat[c, 2], got)
        if c > 0:
            m, g = m + mixacc[0], g + mixacc[1]
        if c < CH - 1:
            mixacc[0], mixacc[1] = m, g
        else:
            mixed[...], gtok[...] = m.astype(BF16), g.astype(BF16)

    stages = [first]
    for s in range(1, half):
        stages.append(functools.partial(rs_hop, step=s))
    stages.append(middle)
    for s in range(1, half):
        stages.append(functools.partial(ag_hop, step=s))
    stages.append(last)
    order = stage_order(len(stages))
    place = {(c, stage): n for n, (c, stage) in enumerate(order)}
    after = [[] for _ in order]
    for c in range(CH):
        over = place[(c, len(stages) - 1)]
        after[min(over + 1, len(order) - 1)].append(functools.partial(weight_grads, c))
        after[min(over + LAG, len(order) - 1)].append(functools.partial(mix, c))
        after[place[(0, 2 + c)]].append(functools.partial(tables, c))
    for n, (c, stage) in enumerate(order):
        if n == len(order) - 1:
            sent(0)
            for i in range(3):
                weight_copy(i).wait_send()
        stages[stage](c)
        for task in after[n]:
            task()

    for c in range(1, CH):
        sent(c)


def finish(*refs):
    ins, outs, sem = refs[:5], refs[5:10], refs[10]
    copies = [pltpu.make_async_copy(src, dst, sem.at[i]) for i, (src, dst) in enumerate(zip(ins, outs))]
    for copy in copies:
        copy.start()
    for copy in copies:
        copy.wait()


def local(tokens, cotangent, route, prob, quota, w_gate, w_up, w_down):
    n_exp = lax.axis_size("expert")
    n_z = lax.axis_size("dp") // 2
    tok_n, feat = tokens.shape
    hid = w_gate.shape[2]
    half = n_z // 2
    n_src = n_exp // 2
    rows = n_src * SL
    zr = rows // n_z
    hh = hid // 2
    vm = pl.BlockSpec(memory_space=pltpu.VMEM)
    hbm = pl.BlockSpec(memory_space=pltpu.HBM)
    sm = pl.BlockSpec(memory_space=pltpu.SMEM)
    dma = pltpu.SemaphoreType.DMA
    shapes = (
        jax.ShapeDtypeStruct((tok_n, feat), BF16),
        jax.ShapeDtypeStruct((tok_n, feat), BF16),
        jax.ShapeDtypeStruct((1, feat, hid), BF16),
        jax.ShapeDtypeStruct((1, feat, hid), BF16),
        jax.ShapeDtypeStruct((1, hid, feat), BF16),
    )
    outs = pl.pallas_call(
        functools.partial(kernel, n_exp, n_z),
        out_shape=tuple(pltpu.VMEM(s.shape, s.dtype) for s in shapes),
        in_specs=[hbm, hbm, vm, vm, sm, hbm, hbm, hbm],
        out_specs=[vm] * 5,
        scratch_shapes=[
            pltpu.VMEM((tok_n, feat), BF16),
            pltpu.VMEM((tok_n, feat), BF16),
            pltpu.VMEM((2 * feat, hid), BF16),
            pltpu.VMEM((2 * feat, hid), BF16),
            pltpu.VMEM((2, hid, feat), BF16),
            pltpu.VMEM((CH, n_exp, 2 * SL, feat), BF16),
            pltpu.VMEM((CH, 2, n_src, 2 * SL, feat), BF16),
            pltpu.VMEM((2, CH, 2 * SL, feat), BF16),
            pltpu.VMEM((2, CH * rows, feat), BF16),
            pltpu.VMEM((2, CH * rows, feat), BF16),
            pltpu.VMEM((CH, n_z, 2, 3 * zr, hh), BF16),
            pltpu.VMEM((CH, 2, 2, half, 3 * zr, hh), BF16),
            pltpu.VMEM((CH, n_z, 2, 3 * zr, hh), BF16),
            pltpu.VMEM((CH, 2, n_src, 2 * SL, feat), BF16),
            pltpu.VMEM((CH, n_exp, 2 * SL, feat), BF16),
            pltpu.VMEM((CH, 3, tok_n, n_exp * 2 * SL), BF16),
            pltpu.VMEM((2, tok_n, feat), F32),
            pltpu.VMEM((2, feat, hid), F32),
            pltpu.VMEM((hid, feat), F32),
            pltpu.VMEM((CH, n_z, 2, 3 * zr, hh), BF16),
            pltpu.VMEM((CH * rows, feat), BF16),
            pltpu.VMEM((CH * rows, feat), BF16),
            dma((2,)),
            dma((3,)), dma((3,)), dma((3,)),
            dma((CH,)), dma((CH,)),
            dma((CH,)), dma((CH, 2, 2, half)),
            dma((CH,)), dma((CH, 2, 2, half)),
            dma((CH,)), dma((CH,)),
            dma((CH, 2)), dma((CH, 2)),
            dma((CH,)), dma((CH,)),
        ],
        compiler_params=pltpu.CompilerParams(
            collective_id=0, has_side_effects=True, vmem_limit_bytes=63000 * 1024
        ),
    )(tokens, cotangent, route.T, prob.T, quota, w_gate, w_up, w_down)
    return pl.pallas_call(
        finish,
        out_shape=shapes,
        in_specs=[vm] * 5,
        out_specs=[hbm] * 5,
        scratch_shapes=[dma((5,))],
        compiler_params=pltpu.CompilerParams(vmem_limit_bytes=8 * 1024 * 1024),
    )(*outs)


def solution(mesh):
    placed = (
        P("expert", "dp"),
        P("expert", "dp"),
        P("expert", None),
        P("expert", None),
        P(),
        P("expert", "dp", None),
        P("expert", "dp", None),
        P("expert", None, "dp"),
    )
    return jax.shard_map(
        local,
        mesh=mesh,
        in_specs=placed,
        out_specs=(
            P("expert", "dp"),
            P("expert", "dp"),
            P("expert", "dp", None),
            P("expert", "dp", None),
            P("expert", None, "dp"),
        ),
        check_vma=False,
    )
```
